32 devices in a mesh: pipe: 4 (over y, core), win: 4 (over z), head: 2 (over x).
Axes of the slice: x: 2, y: 2, z: 4, core: 2. Of those that a mesh axis runs over, the one named last changes fastest.
Arguments:
- stream: bfloat16 [8, 128, 2048], P('head', 'win'), may hold values from -16 to 16
- score_scale: float32 [4, 2048], P('pipe'), may hold values from -12 to 12
- value_weight: bfloat16 [4, 2048, 2048], P('pipe', None, 'head'), may hold values from -0.125 to 0.125
- out_weight: bfloat16 [4, 2048, 2048], P('pipe', 'head'), may hold values from -0.25 to 0.25
Outputs:
- sections: bfloat16 [4, 8, 128, 2048], P('pipe', None, 'win', 'head')
The draws below stay inside these ranges and needn't reach their ends.
All inputs are finite; a program needn't handle non-finite values.
Results may differ from the reference program's by a relative error of at most 0.03.
Values may be sent and summed in bfloat16 or wider, within the bound.
No kernel may reach another device: no remote copies, remote signals or barrier semaphores. Data moves between devices by JAX's collectives and lax.ppermute only.
A program may use at most 64 MiB of HBM per device.

```python
import math
import jax
import jax.numpy as jnp
from jax import lax

HEADS = 16
HEAD_DIM = 128
WIN = 32
ROWS = 8
D = 2048
COLS = 128
SECTIONS = 4
N_HEAD = 2


def scale_pattern(key):
    return 2.0 * jax.random.normal(jax.random.fold_in(key, 11), (SECTIONS, HEADS * HEAD_DIM), jnp.float32)


def draw_score_scale(key, part):
    return jnp.clip(scale_pattern(key), -12.0, 12.0)


def draw_stream(key, part):
    channels = HEADS * HEAD_DIM
    return jnp.clip(jax.random.normal(jax.random.fold_in(key, 14), (ROWS, COLS, channels), jnp.float32), -6.0, 6.0).astype(jnp.bfloat16)


def level_of(stream_key, extent, cuts, smallest, top_value):
    gain = 1.0
    for dim, shards_of in cuts:
        steps = jax.random.uniform(jax.random.fold_in(jax.random.fold_in(stream_key, 6), dim), (shards_of,), jnp.float32, smallest / len(cuts), top_value / len(cuts))
        gain = gain * jnp.repeat(jnp.exp(steps), extent[dim] // shards_of).reshape((-1,) + (1,) * (len(extent) - 1 - dim))
    return gain


def bell_draw(rng, extent, deviation, most, cuts=(), kind=jnp.bfloat16):
    level = level_of(rng, extent, cuts, -0.22, 0.18) if cuts else 1.0
    entries = jax.random.normal(rng, extent, jnp.float32) * deviation * level
    return jnp.minimum(jnp.maximum(entries, -most), most).astype(kind)


def setup_inputs(seed: int = 0) -> dict:
    arg_keys = jax.random.split(jax.random.key(seed), 5)
    stream = draw_stream(jax.random.fold_in(arg_keys[4], 71), 0)
    score_scale = draw_score_scale(jax.random.fold_in(arg_keys[4], 71), 0)
    value_weight = bell_draw(arg_keys[2], (SECTIONS, D, D), D ** -0.5, 0.125, ((0, 4), (2, 2)))
    out_weight = bell_draw(arg_keys[3], (SECTIONS, D, D), (D // 4) ** -0.5, 0.25, ((0, 4), (1, 2)))
    return {"stream": stream, "score_scale": score_scale, "value_weight": value_weight, "out_weight": out_weight}


def attend_all(normed, query_scale, value_matrix):
    window_count = COLS // WIN
    token_count = ROWS * WIN
    normed_f = normed.astype(jnp.float32)
    queries = lax.optimization_barrier((normed_f * query_scale).astype(jnp.bfloat16))
    values = jnp.dot(normed.reshape(ROWS * COLS, D), value_matrix, preferred_element_type=jnp.float32)
    values = lax.optimization_barrier(values.astype(jnp.bfloat16)).reshape(ROWS, COLS, D)
    inv_root = 1.0 / math.sqrt(HEAD_DIM)

    def one_window(window_id):
        first_col = (window_id * WIN).astype(jnp.int32)

        def take_window(tensor):
            window_part = lax.dynamic_slice_in_dim(tensor, first_col, WIN, 1)
            return window_part.reshape(token_count, HEADS, HEAD_DIM).astype(jnp.float32)
        scores = jnp.einsum('qhd,khd->hqk', take_window(queries), take_window(normed)) * inv_root
        attention_probabilities = jax.nn.softmax(scores, axis=-1)
        attention_probabilities = lax.optimization_barrier(attention_probabilities.astype(jnp.bfloat16)).astype(jnp.float32)
        attended = jnp.einsum('hqk,khd->qhd', attention_probabilities, take_window(values))
        return attended.astype(jnp.bfloat16).reshape(ROWS, WIN, D)
    results = lax.map(one_window, jnp.arange(window_count, dtype=jnp.int32))
    return results.transpose(1, 0, 2, 3).reshape(ROWS, COLS, D)

def project_out(attended, out_matrix):
    flattened = attended.reshape(ROWS * COLS, D)
    group_width = D // N_HEAD
    exponent_total = jnp.zeros((ROWS * COLS, D), jnp.float32)
    for group_index in range(N_HEAD):
        lower = group_index * group_width
        piece_term = jnp.dot(flattened[:, lower:lower + group_width], out_matrix[lower:lower + group_width], preferred_element_type=jnp.float32)
        exponent_total = exponent_total + lax.optimization_barrier(piece_term.astype(jnp.bfloat16)).astype(jnp.float32)
    return exponent_total.reshape(ROWS, COLS, D)

def reference(stream, score_scale, value_weight, out_weight):
    current = stream
    collected = []
    for section in range(SECTIONS):
        current_f = current.astype(jnp.float32)
        mean_square = lax.optimization_barrier(jnp.mean(current_f * current_f, axis=2, keepdims=True))
        normed = lax.optimization_barrier((current_f * lax.rsqrt(mean_square + 1e-06)).astype(jnp.bfloat16))
        offset_cols = section % 2 * (WIN // 2)
        aligned = jnp.roll(normed, -offset_cols, axis=1)
        attended = attend_all(aligned, score_scale[section], value_weight[section])
        attended = jnp.roll(attended, offset_cols, axis=1)
        mixture = project_out(attended, out_weight[section])
        updated = (current_f + mixture).astype(jnp.bfloat16)
        current = lax.optimization_barrier(updated)
        collected.append(current)
    return jnp.stack(collected)
```

```python
import functools
import math

import jax
import jax.numpy as jnp
from jax import lax
from jax.experimental import pallas as pl
from jax.experimental.pallas import tpu as pltpu
from jax.sharding import PartitionSpec as P

HEAD_DIM = 128
WIN = 32
HALF = WIN // 2
EPSILON = 1e-06
AXES = ("pipe", "win", "head")
VMEM_LIMIT = 24 * 1024 * 1024

vmem = pl.BlockSpec(memory_space=pltpu.VMEM)
smem = pl.BlockSpec(memory_space=pltpu.SMEM)


def project_kernel(section, chunk_order, n_parts, meta, *refs):
    parts, refs = refs[:n_parts], refs[n_parts:]
    scale, weight, x_ref, q_ref, k_ref, v_ref, u_ref = refs
    channels = q_ref.shape[1]

    @pl.when(meta[0] == section)
    def _():
        first = pl.multiple_of(meta[1] * channels, channels)
        for source, target in enumerate(chunk_order):
            rows = pl.ds(source * HALF, HALF)
            put = pl.ds(target * HALF, HALF)
            total = parts[0][rows, :].astype(jnp.float32)
            for part in parts[1:]:
                total = total + part[rows, :].astype(jnp.float32)
            x = total.astype(x_ref.dtype)
            x_ref[put, :] = x
            wide = x.astype(jnp.float32)
            mean_square = jnp.mean(wide * wide, axis=1, keepdims=True)
            u_ref[put, :] = (wide * lax.rsqrt(mean_square + EPSILON)).astype(u_ref.dtype)
        key = u_ref[:, pl.ds(first, channels)]
        k_ref[...] = key
        q_ref[...] = (key.astype(jnp.float32) * scale[...]).astype(q_ref.dtype)
        v_ref[...] = jnp.dot(
            u_ref[...], weight[...], preferred_element_type=jnp.float32
        ).astype(v_ref.dtype)


def project(section, chunk_order, parts, meta, scale, weight):
    rows, width = parts[0].shape
    channels = weight.shape[1]
    bf16 = jnp.bfloat16
    return pl.pallas_call(
        functools.partial(project_kernel, section, chunk_order, len(parts)),
        out_shape=(
            jax.ShapeDtypeStruct((rows, width), bf16),
            jax.ShapeDtypeStruct((rows, channels), bf16),
            jax.ShapeDtypeStruct((rows, channels), bf16),
            jax.ShapeDtypeStruct((rows, channels), bf16),
        ),
        in_specs=[smem] + [vmem] * (len(parts) + 2),
        out_specs=(vmem,) * 4,
        scratch_shapes=[pltpu.VMEM((rows, width), bf16)],
        compiler_params=pltpu.CompilerParams(vmem_limit_bytes=VMEM_LIMIT),
        cost_estimate=pl.CostEstimate(
            flops=2 * rows * width * channels, bytes_accessed=2 * width * channels, transcendentals=0
        ),
        name="project",
    )(meta, *parts, scale, weight)


def attend_kernel(section, pieces, n_blocks, split, meta, *refs):
    blocks, refs = refs[: 4 * n_blocks], refs[4 * n_blocks :]
    xs, qs, ks, vs = (blocks[i * n_blocks : (i + 1) * n_blocks] for i in range(4))
    weight, refs = refs[0], refs[1:]
    outs, o_ref = refs[:-1], refs[-1]
    channels = qs[0].shape[1]
    width = xs[0].shape[1]
    inv_root = 1.0 / math.sqrt(HEAD_DIM)
    n_head = width // channels

    @pl.when(meta[0] == section)
    def _():
        for head in range(channels // HEAD_DIM):
            lanes = slice(head * HEAD_DIM, (head + 1) * HEAD_DIM)
            q = [qs[block][start : start + size, lanes] for block, start, size in pieces]
            q = jnp.concatenate(q, axis=0) if len(q) > 1 else q[0]
            scores = jnp.concatenate(
                [
                    lax.dot_general(
                        q, k[:, lanes], (((1,), (1,)), ((), ())), preferred_element_type=jnp.float32
                    )
                    for k in ks
                ],
                axis=1,
            )
            scores = scores * inv_root
            weights = jnp.exp(scores - jnp.max(scores, axis=1, keepdims=True))
            weights = (weights / jnp.sum(weights, axis=1, keepdims=True)).astype(jnp.bfloat16)
            attended, at = None, 0
            for v in vs:
                term = jnp.dot(
                    weights[:, at : at + v.shape[0]], v[:, lanes], preferred_element_type=jnp.float32
                )
                attended = term if attended is None else attended + term
                at += v.shape[0]
            o_ref[:, lanes] = attended.astype(o_ref.dtype)
        mine = jnp.where(meta[1] == 0, 1.0, 0.0)
        attended = o_ref[...]
        step = channels if split else min(512, width)
        for column in range(0, width, step):
            if split:
                out = outs[column // step]
                block = lax.rem(meta[1] + column // step, n_head)
                lanes = pl.ds(pl.multiple_of(block * step, step), step)
                put_lanes = slice(0, step)
            else:
                out = outs[0]
                lanes = put_lanes = slice(column, column + step)
            g = jnp.dot(attended, weight[:, lanes], preferred_element_type=jnp.float32)
            at = 0
            for turn, (block, start, size) in enumerate(pieces):
                residual = xs[block][start : start + size, lanes].astype(jnp.float32) * mine
                value = residual + g[at : at + size]
                if len(pieces) > 1:
                    place = lax.rem(meta[1] + len(pieces) - turn, len(pieces)) * size
                    rows = pl.ds(pl.multiple_of(place, size), size)
                else:
                    rows = slice(0, size)
                out[rows, put_lanes] = value.astype(out.dtype)
                at += size


def attend(section, pieces, blocks, meta, weight, split):
    rows = sum(size for _, _, size in pieces)
    channels, width = weight.shape
    keys = sum(block[2].shape[0] for block in blocks)
    n_head = width // channels
    if split:
        out_shape = tuple(jax.ShapeDtypeStruct((rows, channels), jnp.bfloat16) for _ in range(n_head))
    else:
        out_shape = (jax.ShapeDtypeStruct((rows, width), jnp.bfloat16),)
    arrays = [block[i] for i in range(4) for block in blocks]
    return pl.pallas_call(
        functools.partial(attend_kernel, section, pieces, len(blocks), split),
        out_shape=out_shape,
        in_specs=[smem] + [vmem] * (len(arrays) + 1),
        out_specs=(vmem,) * len(out_shape),
        scratch_shapes=[pltpu.VMEM((rows, channels), jnp.bfloat16)],
        compiler_params=pltpu.CompilerParams(vmem_limit_bytes=VMEM_LIMIT),
        cost_estimate=pl.CostEstimate(
            flops=2 * rows * channels * (width + 2 * keys),
            bytes_accessed=2 * width * channels,
            transcendentals=rows * keys * channels // HEAD_DIM,
        ),
        name="attend",
    )(meta, *arrays, weight)


def per_device(stream, score_scale, value_weight, out_weight):
    row_count, col_count, width = stream.shape
    assert col_count == WIN, "one window"
    sections, n_win, n_head = (lax.axis_size(axis) for axis in AXES)
    channels = value_weight.shape[2]
    stage, head = lax.axis_index("pipe"), lax.axis_index("head")
    meta = jnp.stack([stage, head]).astype(jnp.int32)
    scale = lax.dynamic_slice_in_dim(score_scale, head * channels, channels, 1)
    value_cols, out_rows = value_weight[0], out_weight[0]

    def send(value, pairs):
        at = lambda pipe, win, head: (pipe * n_win + win % n_win) * n_head + head % n_head
        return lax.ppermute(value, AXES, [(at(*source), at(*target)) for source, target in pairs])

    places = [(win, group) for win in range(n_win) for group in range(n_head)]

    piece = row_count * HALF
    natural = tuple(
        (chunk % 2) * row_count + chunk // 2 for chunk in range(row_count * col_count // HALF)
    )
    own = stream.reshape(row_count * col_count, width)
    arrived = [own]
    for turn in range(1, n_head):
        arrived.append(send(own, [((0, w, g), (0, w, g + turn)) for w, g in places]))
    blocks = [project(0, natural, [cells], meta, scale, value_cols) for cells in arrived]
    halves = [[(block, half * piece, piece) for block in range(n_head)] for half in range(2)]
    straight = tuple(range(row_count * n_head))
    recorded = [None, None]

    for section in range(sections):
        shift = section % 2
        last = section + 1 == sections
        cross = 0 if last else (1 if shift else -1)
        moved = []
        for half in range(2):
            part = attend(section, halves[half], blocks, meta, out_rows, last)
            if last:
                over = shift if half == 0 else 0
                terms = []
                for turn, block in enumerate(part):
                    if over or turn:
                        block = send(
                            block, [((section, w, g), (section, w + over, g + turn)) for w, g in places]
                        )
                    terms.append(block)
            else:
                over = cross if half == 0 else 0
                terms = [
                    send(part[0], [((section, w, g), (section + 1, w + over, g + turn)) for w, g in places])
                    for turn in range(n_head)
                ]
            moved.append(terms)
        if not last:
            blocks = [
                project(section + 1, straight, terms, meta, scale, value_cols) for terms in moved
            ]
            halves = [[(0, 0, piece * n_head)], [(1, 0, piece * n_head)]]
            for half in range(2):
                mine = lax.dynamic_slice_in_dim(blocks[half][0], head * channels, channels, 1)
                kept = recorded[half]
                recorded[half] = mine if kept is None else jnp.where(stage == section + 1, mine, kept)
    outputs = []
    for half in range(2):
        back = []
        for source in range(1, sections):
            over = source % 2 if half == 0 else 0
            back += [((source, w, g), (source - 1, w + over, g)) for w, g in places]
        earlier = send(recorded[half], back)
        total = sum(term.astype(jnp.float32) for term in moved[half]).astype(jnp.bfloat16)
        total = jnp.where(stage == sections - 1, total, earlier)
        outputs.append(total.reshape(row_count * n_head, HALF, channels))
    return jnp.concatenate(outputs, axis=1)[None]


def solution(mesh):
    placed = (
        P("head", "win", None),
        P("pipe", None),
        P("pipe", None, "head"),
        P("pipe", "head", None),
    )
    return jax.shard_map(
        per_device,
        mesh=mesh,
        in_specs=placed,
        out_specs=P("pipe", None, "win", "head"),
        check_vma=False,
    )
```

```python
import functools
import math

import jax
import jax.numpy as jnp
from jax import lax
from jax.experimental import pallas as pl
from jax.experimental.pallas import tpu as pltpu
from jax.sharding import PartitionSpec as P

HEAD_DIM = 128
WIN = 32
HALF = WIN // 2
EPSILON = 1e-06
AXES = ("pipe", "win", "head")
VMEM_LIMIT = 14 * 1024 * 1024

vmem = pl.BlockSpec(memory_space=pltpu.VMEM)
anywhere = pl.BlockSpec(memory_space=pl.ANY)
MARK = jax.ShapeDtypeStruct((8, 128), jnp.float32)


def project_kernel(section, chunk_order, n_parts, keep, mark, *refs):
    parts, refs = refs[:n_parts], refs[n_parts:]
    scale, weight, refs = refs[0], refs[1], refs[2:]
    before, refs = (refs[0], refs[1:]) if keep == "hand on" else (None, refs)
    x_ref, q_ref, k_ref, v_ref, refs = *refs[:4], refs[4:]
    kept = refs[0] if keep else None
    u_ref = refs[-1]
    channels = q_ref.shape[1]

    @pl.when(lax.axis_index("pipe") == section)
    def _():
        mine = pl.ds(pl.multiple_of(lax.axis_index("head") * channels, channels), channels)
        for source, target in enumerate(chunk_order):
            rows = pl.ds(source * HALF, HALF)
            put = pl.ds(target * HALF, HALF)
            total = parts[0][rows, :].astype(jnp.float32)
            for part in parts[1:]:
                total = total + part[rows, :].astype(jnp.float32)
            x = total.astype(x_ref.dtype)
            x_ref[put, :] = x
            wide = x.astype(jnp.float32)
            mean_square = jnp.mean(wide * wide, axis=1, keepdims=True)
            u_ref[put, :] = (wide * lax.rsqrt(mean_square + EPSILON)).astype(u_ref.dtype)
        key = u_ref[:, mine]
        k_ref[...] = key
        q_ref[...] = (key.astype(jnp.float32) * scale[:, mine]).astype(q_ref.dtype)
        v_ref[...] = jnp.dot(
            u_ref[...], weight[...], preferred_element_type=jnp.float32
        ).astype(v_ref.dtype)
        if keep:
            kept[...] = x_ref[:, mine]

    if keep == "hand on":

        @pl.when(lax.axis_index("pipe") != section)
        def _():
            kept[...] = before[...]


def project(section, chunk_order, parts, mark, scale, weight, before):
    rows, width = parts[0].shape
    channels = weight.shape[1]
    keep = "" if section == 0 else "start" if before is None else "hand on"
    shapes = [(rows, width)] + [(rows, channels)] * (4 if keep else 3)
    arrays = [*parts, scale, weight] + ([before] if keep == "hand on" else [])
    return pl.pallas_call(
        functools.partial(project_kernel, section, chunk_order, len(parts), keep),
        out_shape=tuple(jax.ShapeDtypeStruct(shape, jnp.bfloat16) for shape in shapes) + (MARK,),
        in_specs=[anywhere] + [vmem] * len(arrays),
        out_specs=(vmem,) * len(shapes) + (anywhere,),
        scratch_shapes=[pltpu.VMEM((rows, width), jnp.bfloat16)],
        compiler_params=pltpu.CompilerParams(vmem_limit_bytes=VMEM_LIMIT),
        cost_estimate=pl.CostEstimate(
            flops=2 * rows * width * channels, bytes_accessed=2 * width * channels, transcendentals=0
        ),
        name="project",
    )(mark, *arrays)


def join(values, axis):
    return jnp.concatenate(values, axis=axis) if len(values) > 1 else values[0]


def attend_kernel(section, pieces, n_blocks, split, mark, *refs):
    blocks, refs = refs[: 4 * n_blocks], refs[4 * n_blocks :]
    xs, qs, ks, vs = (blocks[i * n_blocks : (i + 1) * n_blocks] for i in range(4))
    weight, refs = refs[0], refs[1:]
    outs, o_ref = refs[:-2], refs[-1]
    channels = qs[0].shape[1]
    width = xs[0].shape[1]
    inv_root = 1.0 / math.sqrt(HEAD_DIM)
    n_head = width // channels

    @pl.when(lax.axis_index("pipe") == section)
    def _():
        heads = [slice(at, at + HEAD_DIM) for at in range(0, channels, HEAD_DIM)]
        keys = sum(k.shape[0] for k in ks)
        ones = jnp.ones((keys, HEAD_DIM), jnp.bfloat16)
        weights = []
        for lanes in heads:
            q = join([qs[block][start : start + size, lanes] for block, start, size in pieces], 0)
            scores = join(
                [
                    lax.dot_general(
                        q, k[:, lanes], (((1,), (1,)), ((), ())), preferred_element_type=jnp.float32
                    )
                    for k in ks
                ],
                1,
            )
            highest = jnp.max(scores, axis=1, keepdims=True)
            weights.append(jnp.exp((scores - highest) * inv_root).astype(jnp.bfloat16))
        for lanes, weight_of_head in zip(heads, weights):
            v = jnp.concatenate([join([v[:, lanes] for v in vs], 0), ones], axis=1)
            attended = jnp.dot(weight_of_head, v, preferred_element_type=jnp.float32)
            o_ref[:, lanes] = (attended[:, :HEAD_DIM] / attended[:, HEAD_DIM:]).astype(o_ref.dtype)
        mine = jnp.where(lax.axis_index("head") == 0, 1.0, 0.0)
        attended = o_ref[...]
        step = channels if split else min(512, width)
        for column in range(0, width, step):
            if split:
                out = outs[column // step]
                block = lax.rem(lax.axis_index("head") + column // step, n_head)
                lanes = pl.ds(pl.multiple_of(block * step, step), step)
                put_lanes = slice(0, step)
            else:
                out = outs[0]
                lanes = put_lanes = slice(column, column + step)
            g = jnp.dot(attended, weight[:, lanes], preferred_element_type=jnp.float32)
            at = 0
            for turn, (block, start, size) in enumerate(pieces):
                residual = xs[block][start : start + size, lanes].astype(jnp.float32) * mine
                value = residual + g[at : at + size]
                if len(pieces) > 1:
                    place = lax.rem(lax.axis_index("head") + len(pieces) - turn, len(pieces)) * size
                    rows = pl.ds(pl.multiple_of(place, size), size)
                else:
                    rows = slice(0, size)
                out[rows, put_lanes] = value.astype(out.dtype)
                at += size


def attend(section, pieces, blocks, mark, weight, split):
    rows = sum(size for _, _, size in pieces)
    channels, width = weight.shape
    keys = sum(block[2].shape[0] for block in blocks)
    n_head = width // channels
    if split:
        out_shape = tuple(jax.ShapeDtypeStruct((rows, channels), jnp.bfloat16) for _ in range(n_head))
    else:
        out_shape = (jax.ShapeDtypeStruct((rows, width), jnp.bfloat16),)
    arrays = [block[i] for i in range(4) for block in blocks]
    return pl.pallas_call(
        functools.partial(attend_kernel, section, pieces, len(blocks), split),
        out_shape=out_shape + (MARK,),
        in_specs=[anywhere] + [vmem] * (len(arrays) + 1),
        out_specs=(vmem,) * len(out_shape) + (anywhere,),
        scratch_shapes=[pltpu.VMEM((rows, channels), jnp.bfloat16)],
        compiler_params=pltpu.CompilerParams(vmem_limit_bytes=VMEM_LIMIT),
        cost_estimate=pl.CostEstimate(
            flops=2 * rows * channels * (width + 2 * keys),
            bytes_accessed=2 * width * channels,
            transcendentals=rows * keys * channels // HEAD_DIM,
        ),
        name="attend",
    )(mark, *arrays, weight)


def add_kernel(section, mark, *refs):
    @pl.when(lax.axis_index("pipe") == section)
    def _():
        total = refs[0][...].astype(jnp.float32)
        for term in refs[1:-2]:
            total = total + term[...].astype(jnp.float32)
        refs[-2][...] = total.astype(refs[-2].dtype)


def add(section, terms, mark):
    return pl.pallas_call(
        functools.partial(add_kernel, section),
        out_shape=(jax.ShapeDtypeStruct(terms[0].shape, terms[0].dtype), MARK),
        in_specs=[anywhere] + [vmem] * len(terms),
        out_specs=(vmem, anywhere),
        compiler_params=pltpu.CompilerParams(vmem_limit_bytes=VMEM_LIMIT),
        name="add",
    )(mark, *terms)


def finish_kernel(section, *refs):
    sums, backs, out = refs[:2], refs[2:4], refs[4]
    shape = (out.shape[0], HALF, out.shape[2])
    for choice, halves in ((lax.axis_index("pipe") == section, sums), (lax.axis_index("pipe") != section, backs)):

        @pl.when(choice)
        def _():
            for half in range(2):
                out[:, half * HALF : (half + 1) * HALF, :] = halves[half][...].reshape(shape)


def finish(section, row_count, mark, moved, backs):
    channels = backs[0].shape[1]
    sums = []
    for terms in moved:
        total, mark = add(section, terms, mark)
        sums.append(total)
    return pl.pallas_call(
        functools.partial(finish_kernel, section),
        out_shape=jax.ShapeDtypeStruct((row_count, WIN, channels), jnp.bfloat16),
        in_specs=[vmem] * 4,
        out_specs=vmem,
        compiler_params=pltpu.CompilerParams(vmem_limit_bytes=VMEM_LIMIT),
        name="finish",
    )(*sums, *backs)


def after(arrays, mark):
    shapes = tuple(jax.ShapeDtypeStruct(array.shape, array.dtype) for array in arrays)
    return pl.pallas_call(
        lambda *refs: None,
        out_shape=shapes,
        in_specs=[anywhere] * (len(arrays) + 1),
        out_specs=(anywhere,) * len(arrays),
        input_output_aliases={place: place for place in range(len(arrays))},
        compiler_params=pltpu.CompilerParams(vmem_limit_bytes=1024 * 1024),
        name="after",
    )(*arrays, mark)


def per_device(stream, score_scale, value_weight, out_weight):
    row_count, col_count, width = stream.shape
    assert col_count == WIN, "one window"
    sections, n_win, n_head = (lax.axis_size(axis) for axis in AXES)
    value_cols, out_rows = value_weight[0], out_weight[0]
    places = [(win, group) for win in range(n_win) for group in range(n_head)]

    def send(value, start, stop, over=0, turn=0):
        return send_all(value, [(start, stop)], [over], turn)

    def send_all(value, hops, overs, turn=0):
        at = lambda pipe, win, group: (pipe * n_win + win % n_win) * n_head + group % n_head
        pairs = [
            (at(start, win, group), at(stop, win + over, group + turn))
            for (start, stop), over in zip(hops, overs)
            for win, group in places
        ]
        return lax.ppermute(value, AXES, pairs)

    piece = row_count * HALF
    natural = tuple(
        (chunk % 2) * row_count + chunk // 2 for chunk in range(row_count * col_count // HALF)
    )
    own = stream.reshape(row_count * col_count, width)
    arrived = [own] + [send(own, 0, 0, 0, turn) for turn in range(1, n_head)]
    mark = jnp.zeros(MARK.shape, MARK.dtype)
    blocks = []
    for cells in arrived:
        *block, mark = project(0, natural, [cells], mark, score_scale, value_cols, None)
        blocks.append(block)
    halves = [[(block, half * piece, piece) for block in range(n_head)] for half in range(2)]
    straight = tuple(range(row_count * n_head))
    kept = [None, None]

    for section in range(sections):
        shift = section % 2
        last = section + 1 == sections
        moved = []
        for half in range(2):
            *part, mark = attend(section, halves[half], blocks, mark, out_rows, last)
            cross = 0 if half else shift if last else 1 if shift else -1
            if last:
                terms = [
                    send(block, section, section, cross, turn) if cross or turn else block
                    for turn, block in enumerate(part)
                ]
            elif shift and not half:
                terms = [send(part[0], section, section + 1, cross)]
            else:
                terms = [send(part[0], section, section + 1, cross, turn) for turn in range(n_head)]
            moved.append(terms)
        if shift and not last:
            (one,) = after(moved[0], mark)
            moved[0] = [one] + [
                send(one, section + 1, section + 1, 0, turn) for turn in range(1, n_head)
            ]
        if not last:
            blocks = [None, None]
            for half in (1, 0) if shift else (0, 1):
                *blocks[half], kept[half], mark = project(
                    section + 1, straight, moved[half], mark, score_scale, value_cols, kept[half]
                )
            halves = [[(0, 0, piece * n_head)], [(1, 0, piece * n_head)]]
    hops = [(source, source - 1) for source in range(1, sections)]
    kept = after(kept, mark)
    backs = [
        send_all(kept[half], hops, [0 if half else source % 2 for source, _ in hops])
        for half in range(2)
    ]
    return finish(sections - 1, row_count * n_head, mark, moved, backs)[None]


def solution(mesh):
    placed = (
        P("head", "win", None),
        P("pipe", None),
        P("pipe", None, "head"),
        P("pipe", "head", None),
    )
    return jax.shard_map(
        per_device,
        mesh=mesh,
        in_specs=placed,
        out_specs=P("pipe", None, "win", "head"),
        check_vma=False,
    )
```

```python
import functools
import math

import jax
import jax.numpy as jnp
from jax import lax
from jax.experimental import pallas as pl
from jax.experimental.pallas import tpu as pltpu
from jax.sharding import PartitionSpec as P

HEAD_DIM = 128
WIN = 32
HALF = WIN // 2
EPSILON = 1e-06
AXES = ("pipe", "win", "head")
VMEM_LIMIT = 14 * 1024 * 1024

vmem = pl.BlockSpec(memory_space=pltpu.VMEM)
anywhere = pl.BlockSpec(memory_space=pl.ANY)
MARK = jax.ShapeDtypeStruct((8, 128), jnp.float32)


def project_kernel(section, chunk_order, n_parts, keep, mark, *refs):
    parts, refs = refs[:n_parts], refs[n_parts:]
    scale, weight, refs = refs[0], refs[1], refs[2:]
    before, refs = (refs[0], refs[1:]) if keep == "hand on" else (None, refs)
    x_ref, q_ref, k_ref, v_ref, refs = *refs[:4], refs[4:]
    kept = refs[0] if keep else None
    u_ref = refs[-1]
    channels = q_ref.shape[1]

    @pl.when(lax.axis_index("pipe") == section)
    def _():
        mine = pl.ds(pl.multiple_of(lax.axis_index("head") * channels, channels), channels)
        for source, target in enumerate(chunk_order):
            rows = pl.ds(source * HALF, HALF)
            put = pl.ds(target * HALF, HALF)
            total = parts[0][rows, :].astype(jnp.float32)
            for part in parts[1:]:
                total = total + part[rows, :].astype(jnp.float32)
            x = total.astype(x_ref.dtype)
            x_ref[put, :] = x
            wide = x.astype(jnp.float32)
            mean_square = jnp.mean(wide * wide, axis=1, keepdims=True)
            u_ref[put, :] = (wide * lax.rsqrt(mean_square + EPSILON)).astype(u_ref.dtype)
        key = u_ref[:, mine]
        k_ref[...] = key
        q_ref[...] = (key.astype(jnp.float32) * scale[:, mine]).astype(q_ref.dtype)
        v_ref[...] = jnp.dot(
            u_ref[...], weight[...], preferred_element_type=jnp.float32
        ).astype(v_ref.dtype)
        if keep:
            kept[...] = x_ref[:, mine]

    if keep == "hand on":

        @pl.when(lax.axis_index("pipe") != section)
        def _():
            kept[...] = before[...]


def project(section, chunk_order, parts, mark, scale, weight, keep="", before=()):
    rows, width = parts[0].shape
    channels = weight.shape[1]
    shapes = [(rows, width)] + [(rows, channels)] * (4 if keep else 3)
    arrays = [*parts, scale, weight, *before]
    return pl.pallas_call(
        functools.partial(project_kernel, section, chunk_order, len(parts), keep),
        out_shape=tuple(jax.ShapeDtypeStruct(shape, jnp.bfloat16) for shape in shapes) + (MARK,),
        in_specs=[anywhere] + [vmem] * len(arrays),
        out_specs=(vmem,) * len(shapes) + (anywhere,),
        scratch_shapes=[pltpu.VMEM((rows, width), jnp.bfloat16)],
        compiler_params=pltpu.CompilerParams(vmem_limit_bytes=VMEM_LIMIT),
        cost_estimate=pl.CostEstimate(
            flops=2 * rows * width * channels, bytes_accessed=2 * width * channels, transcendentals=0
        ),
        name="project",
    )(mark, *arrays)


def join(values, axis):
    return jnp.concatenate(values, axis=axis) if len(values) > 1 else values[0]


def attend_kernel(section, pieces, n_blocks, split, carry, copies, mark, *refs):
    blocks, refs = refs[: 4 * n_blocks], refs[4 * n_blocks :]
    xs, qs, ks, vs = (blocks[i * n_blocks : (i + 1) * n_blocks] for i in range(4))
    weight, refs = refs[0], refs[1:]
    kept, refs = refs[:carry], refs[carry:]
    outs, o_ref = refs[:-2], refs[-1]
    channels = qs[0].shape[1]
    width = xs[0].shape[1]
    inv_root = 1.0 / math.sqrt(HEAD_DIM)
    n_head = width // channels

    @pl.when(lax.axis_index("pipe") == section)
    def _():
        heads = [slice(at, at + HEAD_DIM) for at in range(0, channels, HEAD_DIM)]
        keys = sum(k.shape[0] for k in ks)
        ones = jnp.ones((keys, HEAD_DIM), jnp.bfloat16)
        weights = []
        for lanes in heads:
            q = join([qs[block][start : start + size, lanes] for block, start, size in pieces], 0)
            scores = join(
                [
                    lax.dot_general(
                        q, k[:, lanes], (((1,), (1,)), ((), ())), preferred_element_type=jnp.float32
                    )
                    for k in ks
                ],
                1,
            )
            highest = jnp.max(scores, axis=1, keepdims=True)
            weights.append(jnp.exp((scores - highest) * inv_root).astype(jnp.bfloat16))
        for lanes, weight_of_head in zip(heads, weights):
            v = jnp.concatenate([join([v[:, lanes] for v in vs], 0), ones], axis=1)
            attended = jnp.dot(weight_of_head, v, preferred_element_type=jnp.float32)
            o_ref[:, lanes] = (attended[:, :HEAD_DIM] / attended[:, HEAD_DIM:]).astype(o_ref.dtype)
        mine = jnp.where(lax.axis_index("head") == 0, 1.0, 0.0)
        attended = o_ref[...]
        step = channels if split else min(512, width)
        for column in range(0, width, step):
            if split:
                out = outs[column // step]
                block = lax.rem(lax.axis_index("head") + column // step, n_head)
                lanes = pl.ds(pl.multiple_of(block * step, step), step)
                put_lanes = slice(0, step)
            else:
                out = outs[0]
                lanes = put_lanes = slice(column, column + step)
            g = jnp.dot(attended, weight[:, lanes], preferred_element_type=jnp.float32)
            at = 0
            for turn, (block, start, size) in enumerate(pieces):
                residual = xs[block][start : start + size, lanes].astype(jnp.float32) * mine
                value = residual + g[at : at + size]
                if len(pieces) > 1:
                    place = lax.rem(lax.axis_index("head") + len(pieces) - turn, len(pieces)) * size
                    rows = pl.ds(pl.multiple_of(place, size), size)
                else:
                    rows = slice(0, size)
                out[rows, put_lanes] = value.astype(out.dtype)
                at += size
        for turn in range(1, copies):
            block = lax.rem(lax.axis_index("head") + turn, n_head)
            lanes = pl.ds(pl.multiple_of(block * channels, channels), channels)
            outs[turn][...] = outs[0][:, lanes]

    if copies:

        @pl.when(lax.axis_index("pipe") != section)
        def _():
            outs[1][...] = kept[0][...]

    elif carry:
        rows = o_ref.shape[0]
        outs[0][rows:, :] = kept[1][...]

        @pl.when(lax.axis_index("pipe") != section)
        def _():
            outs[0][:rows, :] = kept[0][...]


def attend(section, pieces, blocks, mark, weight, split, kept=(), share=False):
    rows = sum(size for _, _, size in pieces)
    channels, width = weight.shape
    keys = sum(block[2].shape[0] for block in blocks)
    n_head = width // channels
    if split:
        out_shape = tuple(
            jax.ShapeDtypeStruct((rows * (2 if kept and turn == 0 else 1), channels), jnp.bfloat16)
            for turn in range(n_head)
        )
    else:
        out_shape = (jax.ShapeDtypeStruct((rows, width), jnp.bfloat16),)
        out_shape += (jax.ShapeDtypeStruct((rows, channels), jnp.bfloat16),) * (n_head - 1 if share else 0)
    arrays = [block[i] for i in range(4) for block in blocks] + [weight, *kept]
    return pl.pallas_call(
        functools.partial(attend_kernel, section, pieces, len(blocks), split, len(kept), n_head if share else 0),
        out_shape=out_shape + (MARK,),
        in_specs=[anywhere] + [vmem] * len(arrays),
        out_specs=(vmem,) * len(out_shape) + (anywhere,),
        scratch_shapes=[pltpu.VMEM((rows, channels), jnp.bfloat16)],
        compiler_params=pltpu.CompilerParams(vmem_limit_bytes=VMEM_LIMIT),
        cost_estimate=pl.CostEstimate(
            flops=2 * rows * channels * (width + 2 * keys),
            bytes_accessed=2 * width * channels,
            transcendentals=rows * keys * channels // HEAD_DIM,
        ),
        name="attend",
    )(mark, *arrays)


def add_kernel(section, n_before, mark, *refs):
    @pl.when(lax.axis_index("pipe") == section)
    def _():
        before, terms, out = refs[:n_before], refs[n_before:-2], refs[-2]
        rows = out.shape[0] - sum(block.shape[0] for block in before)
        total = terms[0][:rows, :].astype(jnp.float32)
        for term in terms[1:]:
            total = total + term[:rows, :].astype(jnp.float32)
        for block in before:
            out[: block.shape[0], :] = block[...]
        out[out.shape[0] - rows :, :] = total.astype(out.dtype)


def add(section, terms, mark, flops=0, before=()):
    rows, width = min(term.shape for term in terms)
    rows += sum(block.shape[0] for block in before)
    return pl.pallas_call(
        functools.partial(add_kernel, section, len(before)),
        out_shape=(jax.ShapeDtypeStruct((rows, width), terms[0].dtype), MARK),
        in_specs=[anywhere] + [vmem] * (len(before) + len(terms)),
        out_specs=(vmem, anywhere),
        compiler_params=pltpu.CompilerParams(vmem_limit_bytes=VMEM_LIMIT),
        cost_estimate=pl.CostEstimate(flops=flops, bytes_accessed=flops // 100, transcendentals=0),
        name="add",
    )(mark, *before, *terms)


def finish_kernel(last, total, second, share, *refs):
    shared, out = refs[:-1], refs[-1]
    shape = (out.shape[0], HALF, out.shape[2])
    rows, channels = shared[0].shape
    stage = lax.axis_index("pipe")
    first_half, second_half = (slice(half * HALF, (half + 1) * HALF) for half in range(2))

    @pl.when(stage == last)
    def _():
        out[:, first_half, :] = total[:rows, :].reshape(shape)
        out[:, second_half, :] = total[rows:, :].reshape(shape)

    @pl.when(stage != last)
    def _():
        out[:, second_half, :] = second[rows:, :].reshape(shape)

    @pl.when((stage < last - 1) & (stage % 2 == 0))
    def _():
        out[:, first_half, :] = shared[0][...].reshape(shape)

    @pl.when((stage < last - 1) & (stage % 2 == 1))
    def _():
        out[:, first_half, :] = second[:rows, :].reshape(shape)

    @pl.when(stage == last - 1)
    def _():
        mine = pl.ds(pl.multiple_of(lax.axis_index("head") * channels, channels), channels)
        value = share[:, mine].astype(jnp.float32)
        for term in shared:
            value = value + term[...].astype(jnp.float32)
        out[:, first_half, :] = value.astype(out.dtype).reshape(shape)


def finish(last, row_count, total, second, share, shared):
    arrays = [total, second, share, *shared]
    return pl.pallas_call(
        functools.partial(finish_kernel, last),
        out_shape=jax.ShapeDtypeStruct((row_count, WIN, total.shape[1]), jnp.bfloat16),
        in_specs=[vmem] * len(arrays),
        out_specs=vmem,
        compiler_params=pltpu.CompilerParams(vmem_limit_bytes=VMEM_LIMIT),
        name="finish",
    )(*arrays)


def after(arrays, *marks):
    shapes = tuple(jax.ShapeDtypeStruct(array.shape, array.dtype) for array in arrays)
    return pl.pallas_call(
        lambda *refs: None,
        out_shape=shapes,
        in_specs=[anywhere] * (len(arrays) + len(marks)),
        out_specs=(anywhere,) * len(arrays),
        input_output_aliases={place: place for place in range(len(arrays))},
        compiler_params=pltpu.CompilerParams(vmem_limit_bytes=1024 * 1024),
        name="after",
    )(*arrays, *marks)


def per_device(stream, score_scale, value_weight, out_weight):
    row_count, col_count, width = stream.shape
    assert col_count == WIN, "one window"
    sections, n_win, n_head = (lax.axis_size(axis) for axis in AXES)
    assert sections % 2 == 0, "section pairs"
    value_cols, out_rows = value_weight[0], out_weight[0]
    places = [(win, group) for win in range(n_win) for group in range(n_head)]

    def send(value, start, stop, over=0, turn=0):
        return send_all(value, [(start, stop, over, turn)])

    def send_all(value, hops):
        at = lambda pipe, win, group: (pipe * n_win + win % n_win) * n_head + group % n_head
        pairs = [
            (at(start, win, group), at(stop, win + over, group + turn))
            for start, stop, over, turn in hops
            for win, group in places
        ]
        return lax.ppermute(value, AXES, pairs)

    piece = row_count * HALF
    natural = tuple(
        (chunk % 2) * row_count + chunk // 2 for chunk in range(row_count * col_count // HALF)
    )
    own = stream.reshape(row_count * col_count, width)
    arrived = [own] + [send(own, 0, 0, 0, turn) for turn in range(1, n_head)]
    mark = jnp.zeros(MARK.shape, MARK.dtype)
    blocks = []
    for cells in arrived:
        *block, mark = project(0, natural, [cells], mark, score_scale, value_cols)
        blocks.append(block)
    halves = [[(block, half * piece, piece) for block in range(n_head)] for half in range(2)]
    straight = tuple(range(row_count * n_head))
    kept = [None, None]
    back = [(source, source - 1, 0, 0) for source in range(1, sections)]

    for section in range(sections):
        shift = section % 2
        last = section + 1 == sections
        idle = (section + 2) % sections
        moved = []
        for half in range(2):
            share = section + 2 == sections and not half
            carried = kept[:1] if share else kept if last and half else []
            if last and half:
                (mark,) = after([mark], *early)
            *part, mark = attend(section, halves[half], blocks, mark, out_rows, last, carried, share)
            if share:
                own_share, *shared = part
            cross = 0 if half else shift if last else 1 if shift else -1
            if last and half:
                terms = [send(part[turn], section, section - 1, 0, turn) for turn in range(1, n_head)]
                terms += [send_all(part[0], back)]
            elif last:
                terms = [send(part[turn], section, section - 1, cross, turn) for turn in range(n_head)]
            elif shift and not half:
                terms = [send(part[0], section, idle, cross)]
            elif shift:
                terms = [send(part[0], section, section - 1, 0, turn) for turn in range(n_head)]
            else:
                terms = [send(part[0], section, section + 1, cross, turn) for turn in range(n_head)]
            moved.append(terms)
        if shift and not last:
            (one,) = after(moved[0], mark)
            moved[0] = [send(one, idle, section + 1, 0, turn) for turn in range(n_head)]
            total, mark = add(section - 1, moved[1], mark)
            moved[1] = [send(total, section - 1, section + 1)]
        if section + 2 == sections:
            across = [(source, source - 1, 1, 0) for source in range(1, section, 2)]
            early = [
                send_all(block, ([] if turn else across) + [(section, section, 0, turn + 1)])
                for turn, block in enumerate(after(shared, mark))
            ]
        if not last:
            blocks = [None, None]
            for half in range(2):
                keep = "" if section + 2 == sections and not half else "hand on" if section else "start"
                before = [kept[half]] if keep == "hand on" else []
                *blocks[half], mark = project(
                    section + 1, straight, moved[half], mark, score_scale, value_cols, keep, before
                )
                if keep:
                    *blocks[half], kept[half] = blocks[half]
            halves = [[(0, 0, piece * n_head)], [(1, 0, piece * n_head)]]
    first, mark = add(sections - 2, moved[0], mark, 4 * 10**9)
    second, mark = add(sections - 2, moved[1][:-1], mark, 4 * 10**9)
    total, mark = add(sections - 2, [second, moved[1][-1]], mark, 0, (first,))
    total = send(total, sections - 2, sections - 1)
    return finish(sections - 1, row_count * n_head, total, moved[1][-1], own_share, early)[None]


def solution(mesh):
    placed = (
        P("head", "win", None),
        P("pipe", None),
        P("pipe", None, "head"),
        P("pipe", "head", None),
    )
    return jax.shard_map(
        per_device,
        mesh=mesh,
        in_specs=placed,
        out_specs=P("pipe", None, "win", "head"),
        check_vma=False,
    )
```

```python
import functools
import math

import jax
import jax.numpy as jnp
from jax import lax
from jax.experimental import pallas as pl
from jax.experimental.pallas import tpu as pltpu
from jax.sharding import PartitionSpec as P

HEAD_DIM = 128
WIN = 32
HALF = WIN // 2
EPSILON = 1e-06
AXES = ("pipe", "win", "head")
VMEM_LIMIT = 14 * 1024 * 1024

vmem = pl.BlockSpec(memory_space=pltpu.VMEM)
anywhere = pl.BlockSpec(memory_space=pl.ANY)
MARK = jax.ShapeDtypeStruct((8, 128), jnp.float32)


def project_kernel(section, chunk_order, n_parts, keep, first_row, mark, *refs):
    parts, refs = refs[:n_parts], refs[n_parts:]
    scale, weight, refs = refs[0], refs[1], refs[2 + 2 * (first_row > 0) :]
    before, refs = (refs[0], refs[1:]) if keep == "hand on" else (None, refs)
    x_ref, q_ref, k_ref, v_ref, refs = *refs[:4], refs[4:]
    kept = refs[0] if keep else None
    u_ref = refs[-1]
    channels = q_ref.shape[1]

    @pl.when(lax.axis_index("pipe") == section)
    def _():
        mine = pl.ds(pl.multiple_of(lax.axis_index("head") * channels, channels), channels)
        for source, target in enumerate(chunk_order):
            rows = pl.ds(source * HALF, HALF)
            put = pl.ds(target * HALF, HALF)
            total = parts[0][rows, :].astype(jnp.float32)
            for part in parts[1:]:
                total = total + part[rows, :].astype(jnp.float32)
            x = total.astype(x_ref.dtype)
            x_ref[put, :] = x
            wide = x.astype(jnp.float32)
            mean_square = jnp.mean(wide * wide, axis=1, keepdims=True)
            u_ref[put, :] = (wide * lax.rsqrt(mean_square + EPSILON)).astype(u_ref.dtype)
        key = u_ref[:, mine]
        here = slice(first_row, first_row + u_ref.shape[0])
        k_ref[here, :] = key
        q_ref[...] = (key.astype(jnp.float32) * scale[:, mine]).astype(q_ref.dtype)
        v_ref[here, :] = jnp.dot(
            u_ref[...], weight[...], preferred_element_type=jnp.float32
        ).astype(v_ref.dtype)
        if keep:
            kept[...] = x_ref[:, mine]

    if keep == "hand on":

        @pl.when(lax.axis_index("pipe") != section)
        def _():
            kept[...] = before[...]


def project(section, chunk_order, parts, mark, scale, weight, first_row, total_rows, filled, keep="", before=()):
    rows, width = parts[0].shape
    channels = weight.shape[1]
    shapes = [(rows, width), (rows, channels)] + [(total_rows, channels)] * 2
    shapes += [(rows, channels)] * (1 if keep else 0)
    arrays = [*parts, scale, weight, *filled, *before]
    at = 1 + len(parts) + 2
    return pl.pallas_call(
        functools.partial(project_kernel, section, chunk_order, len(parts), keep, first_row),
        out_shape=tuple(jax.ShapeDtypeStruct(shape, jnp.bfloat16) for shape in shapes) + (MARK,),
        in_specs=[anywhere] + [vmem] * len(arrays),
        out_specs=(vmem,) * len(shapes) + (anywhere,),
        input_output_aliases={at: 2, at + 1: 3} if filled else {},
        scratch_shapes=[pltpu.VMEM((rows, width), jnp.bfloat16)],
        compiler_params=pltpu.CompilerParams(vmem_limit_bytes=VMEM_LIMIT),
        cost_estimate=pl.CostEstimate(
            flops=2 * rows * width * channels, bytes_accessed=2 * width * channels, transcendentals=0
        ),
        name="project",
    )(mark, *arrays)


def join(values, axis):
    return jnp.concatenate(values, axis=axis) if len(values) > 1 else values[0]


def attend_kernel(section, pieces, n_blocks, split, carry, copies, mark, k, v, *refs):
    xs, qs, refs = refs[:n_blocks], refs[n_blocks : 2 * n_blocks], refs[2 * n_blocks :]
    weight, refs = refs[0], refs[1:]
    kept, refs = refs[:carry], refs[carry:]
    outs, o_ref = refs[:-2], refs[-1]
    channels = qs[0].shape[1]
    width = xs[0].shape[1]
    inv_root = 1.0 / math.sqrt(HEAD_DIM)
    n_head = width // channels

    @pl.when(lax.axis_index("pipe") == section)
    def _():
        heads = [slice(at, at + HEAD_DIM) for at in range(0, channels, HEAD_DIM)]
        ones = jnp.ones((v.shape[0], HEAD_DIM), jnp.bfloat16)
        weights = []
        for lanes in heads:
            q = join([qs[block][start : start + size, lanes] for block, start, size in pieces], 0)
            scores = lax.dot_general(
                q, k[:, lanes], (((1,), (1,)), ((), ())), preferred_element_type=jnp.float32
            )
            highest = jnp.max(scores, axis=1, keepdims=True)
            weights.append(jnp.exp((scores - highest) * inv_root).astype(jnp.bfloat16))
        for lanes, weight_of_head in zip(heads, weights):
            values = jnp.concatenate([v[:, lanes], ones], axis=1)
            attended = jnp.dot(weight_of_head, values, preferred_element_type=jnp.float32)
            o_ref[:, lanes] = (attended[:, :HEAD_DIM] / attended[:, HEAD_DIM:]).astype(o_ref.dtype)
        mine = jnp.where(lax.axis_index("head") == 0, 1.0, 0.0)
        attended = o_ref[...]
        step = channels if split else min(512, width)
        for column in range(0, width, step):
            if split:
                out = outs[column // step]
                block = lax.rem(lax.axis_index("head") + column // step, n_head)
                lanes = pl.ds(pl.multiple_of(block * step, step), step)
                put_lanes = slice(0, step)
            else:
                out = outs[0]
                lanes = put_lanes = slice(column, column + step)
            g = jnp.dot(attended, weight[:, lanes], preferred_element_type=jnp.float32)
            at = 0
            for turn, (block, start, size) in enumerate(pieces):
                residual = xs[block][start : start + size, lanes].astype(jnp.float32) * mine
                value = residual + g[at : at + size]
                if len(pieces) > 1:
                    place = lax.rem(lax.axis_index("head") + len(pieces) - turn, len(pieces)) * size
                    rows = pl.ds(pl.multiple_of(place, size), size)
                else:
                    rows = slice(0, size)
                out[rows, put_lanes] = value.astype(out.dtype)
                at += size
        for turn in range(1, copies):
            block = lax.rem(lax.axis_index("head") + turn, n_head)
            lanes = pl.ds(pl.multiple_of(block * channels, channels), channels)
            outs[turn][...] = outs[0][:, lanes]

    if copies:

        @pl.when(lax.axis_index("pipe") != section)
        def _():
            outs[1][...] = kept[0][...]

    elif carry:
        rows = o_ref.shape[0]
        outs[0][rows:, :] = kept[1][...]

        @pl.when(lax.axis_index("pipe") != section)
        def _():
            outs[0][:rows, :] = kept[0][...]


def attend(section, pieces, blocks, mark, weight, split, kept=(), share=False):
    rows = sum(size for _, _, size in pieces)
    channels, width = weight.shape
    keys, values = blocks[-1][2:]
    n_head = width // channels
    if split:
        out_shape = tuple(
            jax.ShapeDtypeStruct((rows * (2 if kept and turn == 0 else 1), channels), jnp.bfloat16)
            for turn in range(n_head)
        )
    else:
        out_shape = (jax.ShapeDtypeStruct((rows, width), jnp.bfloat16),)
        out_shape += (jax.ShapeDtypeStruct((rows, channels), jnp.bfloat16),) * (n_head - 1 if share else 0)
    arrays = [keys, values] + [block[i] for i in range(2) for block in blocks] + [weight, *kept]
    return pl.pallas_call(
        functools.partial(attend_kernel, section, pieces, len(blocks), split, len(kept), n_head if share else 0),
        out_shape=out_shape + (MARK,),
        in_specs=[anywhere] + [vmem] * len(arrays),
        out_specs=(vmem,) * len(out_shape) + (anywhere,),
        scratch_shapes=[pltpu.VMEM((rows, channels), jnp.bfloat16)],
        compiler_params=pltpu.CompilerParams(vmem_limit_bytes=VMEM_LIMIT),
        cost_estimate=pl.CostEstimate(
            flops=2 * rows * channels * (width + 2 * keys.shape[0]),
            bytes_accessed=2 * width * channels,
            transcendentals=rows * keys.shape[0] * channels // HEAD_DIM,
        ),
        name="attend",
    )(mark, *arrays)


def add_kernel(section, n_before, mark, *refs):
    @pl.when(lax.axis_index("pipe") == section)
    def _():
        before, terms, out = refs[:n_before], refs[n_before:-2], refs[-2]
        rows = out.shape[0] - sum(block.shape[0] for block in before)
        total = terms[0][:rows, :].astype(jnp.float32)
        for term in terms[1:]:
            total = total + term[:rows, :].astype(jnp.float32)
        for block in before:
            out[: block.shape[0], :] = block[...]
        out[out.shape[0] - rows :, :] = total.astype(out.dtype)


def add(section, terms, mark, flops=0, before=()):
    rows, width = min(term.shape for term in terms)
    rows += sum(block.shape[0] for block in before)
    return pl.pallas_call(
        functools.partial(add_kernel, section, len(before)),
        out_shape=(jax.ShapeDtypeStruct((rows, width), terms[0].dtype), MARK),
        in_specs=[anywhere] + [vmem] * (len(before) + len(terms)),
        out_specs=(vmem, anywhere),
        compiler_params=pltpu.CompilerParams(vmem_limit_bytes=VMEM_LIMIT),
        cost_estimate=pl.CostEstimate(flops=flops, bytes_accessed=flops // 100, transcendentals=0),
        name="add",
    )(mark, *before, *terms)


def finish_kernel(last, total, second, share, *refs):
    shared, out = refs[:-1], refs[-1]
    shape = (out.shape[0], HALF, out.shape[2])
    rows, channels = shared[0].shape
    stage = lax.axis_index("pipe")
    first_half, second_half = (slice(half * HALF, (half + 1) * HALF) for half in range(2))

    @pl.when(stage == last)
    def _():
        out[:, first_half, :] = total[:rows, :].reshape(shape)
        out[:, second_half, :] = total[rows:, :].reshape(shape)

    @pl.when(stage != last)
    def _():
        out[:, second_half, :] = second[rows:, :].reshape(shape)

    @pl.when((stage < last - 1) & (stage % 2 == 0))
    def _():
        out[:, first_half, :] = shared[0][...].reshape(shape)

    @pl.when((stage < last - 1) & (stage % 2 == 1))
    def _():
        out[:, first_half, :] = second[:rows, :].reshape(shape)

    @pl.when(stage == last - 1)
    def _():
        mine = pl.ds(pl.multiple_of(lax.axis_index("head") * channels, channels), channels)
        value = share[:, mine].astype(jnp.float32)
        for term in shared:
            value = value + term[...].astype(jnp.float32)
        out[:, first_half, :] = value.astype(out.dtype).reshape(shape)


def finish(last, row_count, total, second, share, shared):
    arrays = [total, second, share, *shared]
    return pl.pallas_call(
        functools.partial(finish_kernel, last),
        out_shape=jax.ShapeDtypeStruct((row_count, WIN, total.shape[1]), jnp.bfloat16),
        in_specs=[vmem] * len(arrays),
        out_specs=vmem,
        compiler_params=pltpu.CompilerParams(vmem_limit_bytes=VMEM_LIMIT),
        name="finish",
    )(*arrays)


def new_mark():
    return pl.pallas_call(
        lambda ref: None,
        out_shape=MARK,
        out_specs=anywhere,
        compiler_params=pltpu.CompilerParams(vmem_limit_bytes=1024 * 1024),
        name="new_mark",
    )()


def after(arrays, *marks):
    shapes = tuple(jax.ShapeDtypeStruct(array.shape, array.dtype) for array in arrays)
    return pl.pallas_call(
        lambda *refs: None,
        out_shape=shapes,
        in_specs=[anywhere] * (len(arrays) + len(marks)),
        out_specs=(anywhere,) * len(arrays),
        input_output_aliases={place: place for place in range(len(arrays))},
        compiler_params=pltpu.CompilerParams(vmem_limit_bytes=1024 * 1024),
        name="after",
    )(*arrays, *marks)


def per_device(stream, score_scale, value_weight, out_weight):
    row_count, col_count, width = stream.shape
    assert col_count == WIN, "one window"
    sections, n_win, n_head = (lax.axis_size(axis) for axis in AXES)
    assert sections % 2 == 0, "section pairs"
    value_cols, out_rows = value_weight[0], out_weight[0]
    places = [(win, group) for win in range(n_win) for group in range(n_head)]

    def send(value, start, stop, over=0, turn=0):
        return send_all(value, [(start, stop, over, turn)])

    def send_all(value, hops):
        at = lambda pipe, win, group: (pipe * n_win + win % n_win) * n_head + group % n_head
        pairs = [
            (at(start, win, group), at(stop, win + over, group + turn))
            for start, stop, over, turn in hops
            for win, group in places
        ]
        return lax.ppermute(value, AXES, pairs)

    piece = row_count * HALF
    natural = tuple(
        (chunk % 2) * row_count + chunk // 2 for chunk in range(row_count * col_count // HALF)
    )
    own = stream.reshape(row_count * col_count, width)
    arrived = [own] + [send(own, 0, 0, 0, turn) for turn in range(1, n_head)]
    mark = new_mark()
    blocks, filled = [], ()
    for turn, cells in enumerate(arrived):
        *block, mark = project(
            0, natural, [cells], mark, score_scale, value_cols, turn * own.shape[0], n_head * own.shape[0], filled
        )
        blocks.append(block)
        filled = block[2:]
    halves = [[(block, half * piece, piece) for block in range(n_head)] for half in range(2)]
    straight = tuple(range(row_count * n_head))
    kept = [None, None]
    back = [(source, source - 1, 0, 0) for source in range(1, sections)]

    for section in range(sections):
        shift = section % 2
        last = section + 1 == sections
        idle = (section + 2) % sections
        moved = []
        for half in range(2):
            share = section + 2 == sections and not half
            carried = kept[:1] if share else kept if last and half else []
            if last and half:
                (mark,) = after([mark], *early)
            *part, mark = attend(section, halves[half], blocks, mark, out_rows, last, carried, share)
            if share:
                own_share, *shared = part
            cross = 0 if half else shift if last else 1 if shift else -1
            if last and half:
                terms = [send(part[turn], section, section - 1, 0, turn) for turn in range(1, n_head)]
                terms += [send_all(part[0], back)]
            elif last:
                terms = [send(part[turn], section, section - 1, cross, turn) for turn in range(n_head)]
            elif shift and not half:
                terms = [send(part[0], section, idle, cross)]
            elif shift:
                terms = [send(part[0], section, section - 1, 0, turn) for turn in range(n_head)]
            else:
                terms = [send(part[0], section, section + 1, cross, turn) for turn in range(n_head)]
            moved.append(terms)
        if shift and not last:
            (one,) = after(moved[0], mark)
            moved[0] = [send(one, idle, section + 1, 0, turn) for turn in range(n_head)]
            total, mark = add(section - 1, moved[1], mark)
            moved[1] = [send(total, section - 1, section + 1)]
        if section + 2 == sections:
            across = [(source, source - 1, 1, 0) for source in range(1, section, 2)]
            early = [
                send_all(block, ([] if turn else across) + [(section, section, 0, turn + 1)])
                for turn, block in enumerate(after(shared, mark))
            ]
        if not last:
            blocks, filled, rows = [], (), piece * n_head
            for half in range(2):
                keep = "" if section + 2 == sections and not half else "hand on" if section else "start"
                before = [kept[half]] if keep == "hand on" else []
                *block, mark = project(
                    section + 1,
                    straight,
                    moved[half],
                    mark,
                    score_scale,
                    value_cols,
                    half * rows,
                    2 * rows,
                    filled,
                    keep,
                    before,
                )
                if keep:
                    *block, kept[half] = block
                blocks.append(block)
                filled = block[2:]
            halves = [[(0, 0, piece * n_head)], [(1, 0, piece * n_head)]]
    *across, mark = after([*moved[0][1:], mark])
    second, mark = add(sections - 2, moved[1][:-1], mark, 4 * 10**9)
    first, mark = add(sections - 2, [moved[0][0], *across], mark, 4 * 10**9)
    total, mark = add(sections - 2, [second, moved[1][-1]], mark, 0, (first,))
    total = send(total, sections - 2, sections - 1)
    return finish(sections - 1, row_count * n_head, total, moved[1][-1], own_share, early)[None]


def solution(mesh):
    placed = (
        P("head", "win", None),
        P("pipe", None),
        P("pipe", None, "head"),
        P("pipe", "head", None),
    )
    return jax.shard_map(
        per_device,
        mesh=mesh,
        in_specs=placed,
        out_specs=P("pipe", None, "win", "head"),
        check_vma=False,
    )
```

```python
import functools
import math

import jax
import jax.numpy as jnp
from jax import lax
from jax.experimental import pallas as pl
from jax.experimental.pallas import tpu as pltpu
from jax.sharding import PartitionSpec as P

HEAD_DIM = 128
WIN = 32
HALF = WIN // 2
EPSILON = 1e-06
AXES = ("pipe", "win", "head")
VMEM_LIMIT = 14 * 1024 * 1024

vmem = pl.BlockSpec(memory_space=pltpu.VMEM)
anywhere = pl.BlockSpec(memory_space=pl.ANY)
MARK = jax.ShapeDtypeStruct((8, 128), jnp.float32)


def project_kernel(section, chunk_order, n_parts, n_filled, first_row, keep_row, mark, *refs):
    parts, scale, weight = refs[:n_parts], refs[n_parts], refs[n_parts + 1]
    x_ref, q_ref, k_ref, v_ref, *kept, _ = refs[n_parts + 2 + n_filled :]
    channels = q_ref.shape[1]
    rows_here = len(chunk_order) * HALF

    @pl.when(lax.axis_index("pipe") == section)
    def _():
        mine = pl.ds(pl.multiple_of(lax.axis_index("head") * channels, channels), channels)
        inverse = [None] * len(chunk_order)
        for source, target in enumerate(chunk_order):
            rows = pl.ds(source * HALF, HALF)
            put = pl.ds(target * HALF, HALF)
            total = parts[0][rows, :].astype(jnp.float32)
            for part in parts[1:]:
                total = total + part[rows, :].astype(jnp.float32)
            x = total.astype(x_ref.dtype)
            x_ref[put, :] = x
            wide = x.astype(jnp.float32)
            mean_square = jnp.mean(wide * wide, axis=1, keepdims=True)
            inverse[target] = lax.rsqrt(mean_square + EPSILON)
        inverse = jnp.concatenate(inverse, axis=0)
        here = slice(first_row, first_row + rows_here)
        values = jnp.dot(x_ref[...], weight[...], preferred_element_type=jnp.float32)
        v_ref[here, :] = (values * inverse).astype(v_ref.dtype)
        key = (x_ref[:, mine].astype(jnp.float32) * inverse).astype(k_ref.dtype)
        k_ref[here, :] = key
        q_ref[...] = (key.astype(jnp.float32) * scale[:, mine]).astype(q_ref.dtype)
        for target in kept:
            target[keep_row : keep_row + rows_here, :] = x_ref[:, mine]


def project(section, chunk_order, parts, mark, scale, weight, first_row, total_rows, filled, kept=None, keep_rows=0):
    rows, width = parts[0].shape
    channels = weight.shape[1]
    shapes = [(rows, width), (rows, channels)] + [(total_rows, channels)] * 2
    shapes += [(keep_rows, channels)] if keep_rows else []
    arrays = [*parts, scale, weight, *filled] + ([] if kept is None else [kept])
    at = 1 + len(parts) + 2
    aliases = {at: 2, at + 1: 3} if filled else {}
    if kept is not None:
        aliases[len(arrays)] = 4
    keep_row = first_row if keep_rows > rows else 0
    return pl.pallas_call(
        functools.partial(
            project_kernel, section, chunk_order, len(parts), len(arrays) - at + 1, first_row, keep_row
        ),
        out_shape=tuple(jax.ShapeDtypeStruct(shape, jnp.bfloat16) for shape in shapes) + (MARK,),
        in_specs=[anywhere] + [vmem] * len(arrays),
        out_specs=(vmem,) * len(shapes) + (anywhere,),
        input_output_aliases=aliases,
        compiler_params=pltpu.CompilerParams(vmem_limit_bytes=VMEM_LIMIT),
        cost_estimate=pl.CostEstimate(
            flops=2 * rows * width * channels, bytes_accessed=2 * width * channels, transcendentals=0
        ),
        name="project",
    )(mark, *arrays)


def join(values, axis):
    return jnp.concatenate(values, axis=axis) if len(values) > 1 else values[0]


def attend_kernel(section, pieces, n_blocks, split, carry, copies, mark, k, v, *refs):
    xs, qs, refs = refs[:n_blocks], refs[n_blocks : 2 * n_blocks], refs[2 * n_blocks :]
    weight, refs = refs[0], refs[1:]
    kept, refs = refs[:carry], refs[carry:]
    outs, o_ref = refs[:-2], refs[-1]
    channels = qs[0].shape[1]
    width = xs[0].shape[1]
    inv_root = 1.0 / math.sqrt(HEAD_DIM)
    n_head = width // channels

    @pl.when(lax.axis_index("pipe") == section)
    def _():
        heads = [slice(at, at + HEAD_DIM) for at in range(0, channels, HEAD_DIM)]
        ones = jnp.ones((v.shape[0], HEAD_DIM), jnp.bfloat16)
        weights = []
        for lanes in heads:
            q = join([qs[block][start : start + size, lanes] for block, start, size in pieces], 0)
            scores = lax.dot_general(
                q, k[:, lanes], (((1,), (1,)), ((), ())), preferred_element_type=jnp.float32
            )
            highest = jnp.max(scores, axis=1, keepdims=True)
            weights.append(jnp.exp((scores - highest) * inv_root).astype(jnp.bfloat16))
        for lanes, weight_of_head in zip(heads, weights):
            values = jnp.concatenate([v[:, lanes], ones], axis=1)
            attended = jnp.dot(weight_of_head, values, preferred_element_type=jnp.float32)
            o_ref[:, lanes] = (attended[:, :HEAD_DIM] / attended[:, HEAD_DIM:]).astype(o_ref.dtype)
        mine = jnp.where(lax.axis_index("head") == 0, 1.0, 0.0)
        attended = o_ref[...]
        step = channels if split else min(512, width)
        for column in range(0, width, step):
            if split:
                out = outs[column // step]
                block = lax.rem(lax.axis_index("head") + column // step, n_head)
                lanes = pl.ds(pl.multiple_of(block * step, step), step)
                put_lanes = slice(0, step)
            else:
                out = outs[0]
                lanes = put_lanes = slice(column, column + step)
            g = jnp.dot(attended, weight[:, lanes], preferred_element_type=jnp.float32)
            at = 0
            for turn, (block, start, size) in enumerate(pieces):
                residual = xs[block][start : start + size, lanes].astype(jnp.float32) * mine
                value = residual + g[at : at + size]
                if len(pieces) > 1:
                    place = lax.rem(lax.axis_index("head") + len(pieces) - turn, len(pieces)) * size
                    rows = pl.ds(pl.multiple_of(place, size), size)
                else:
                    rows = slice(0, size)
                out[rows, put_lanes] = value.astype(out.dtype)
                at += size
        for turn in range(1, copies):
            block = lax.rem(lax.axis_index("head") + turn, n_head)
            lanes = pl.ds(pl.multiple_of(block * channels, channels), channels)
            outs[turn][...] = outs[0][:, lanes]

    if copies:

        @pl.when(lax.axis_index("pipe") != section)
        def _():
            outs[1][...] = kept[0][: o_ref.shape[0], :]

    elif carry:
        outs[0][o_ref.shape[0] :, :] = kept[0][...]


def attend(section, pieces, blocks, mark, weight, split, kept=(), share=False):
    rows = sum(size for _, _, size in pieces)
    channels, width = weight.shape
    keys, values = blocks[-1][2:]
    n_head = width // channels
    if split:
        out_shape = tuple(
            jax.ShapeDtypeStruct((rows * (2 if kept and turn == 0 else 1), channels), jnp.bfloat16)
            for turn in range(n_head)
        )
    else:
        out_shape = (jax.ShapeDtypeStruct((rows, width), jnp.bfloat16),)
        out_shape += (jax.ShapeDtypeStruct((rows, channels), jnp.bfloat16),) * (n_head - 1 if share else 0)
    arrays = [keys, values] + [block[i] for i in range(2) for block in blocks] + [weight, *kept]
    return pl.pallas_call(
        functools.partial(attend_kernel, section, pieces, len(blocks), split, len(kept), n_head if share else 0),
        out_shape=out_shape + (MARK,),
        in_specs=[anywhere] + [vmem] * len(arrays),
        out_specs=(vmem,) * len(out_shape) + (anywhere,),
        scratch_shapes=[pltpu.VMEM((rows, channels), jnp.bfloat16)],
        compiler_params=pltpu.CompilerParams(vmem_limit_bytes=VMEM_LIMIT),
        cost_estimate=pl.CostEstimate(
            flops=2 * rows * channels * (width + 2 * keys.shape[0]),
            bytes_accessed=2 * width * channels,
            transcendentals=rows * keys.shape[0] * channels // HEAD_DIM,
        ),
        name="attend",
    )(mark, *arrays)


def add_kernel(section, n_before, mark, *refs):
    @pl.when(lax.axis_index("pipe") == section)
    def _():
        before, terms, out = refs[:n_before], refs[n_before:-2], refs[-2]
        rows = out.shape[0] - sum(block.shape[0] for block in before)
        total = terms[0][:rows, :].astype(jnp.float32)
        for term in terms[1:]:
            total = total + term[:rows, :].astype(jnp.float32)
        for block in before:
            out[: block.shape[0], :] = block[...]
        out[out.shape[0] - rows :, :] = total.astype(out.dtype)


def add(section, terms, mark, flops=0, before=()):
    rows, width = min(term.shape for term in terms)
    rows += sum(block.shape[0] for block in before)
    return pl.pallas_call(
        functools.partial(add_kernel, section, len(before)),
        out_shape=(jax.ShapeDtypeStruct((rows, width), terms[0].dtype), MARK),
        in_specs=[anywhere] + [vmem] * (len(before) + len(terms)),
        out_specs=(vmem, anywhere),
        compiler_params=pltpu.CompilerParams(vmem_limit_bytes=VMEM_LIMIT),
        cost_estimate=pl.CostEstimate(flops=flops, bytes_accessed=flops // 100, transcendentals=0),
        name="add",
    )(mark, *before, *terms)


def finish_kernel(last, total, second, given, share, *refs):
    shared, out = refs[:-1], refs[-1]
    shape = (out.shape[0], HALF, out.shape[2])
    rows, channels = shared[0].shape
    stage = lax.axis_index("pipe")
    first_half, second_half = (slice(half * HALF, (half + 1) * HALF) for half in range(2))

    @pl.when(stage == last)
    def _():
        out[:, first_half, :] = total[:rows, :].reshape(shape)
        out[:, second_half, :] = total[rows:, :].reshape(shape)

    @pl.when(stage == last - 1)
    def _():
        mine = pl.ds(pl.multiple_of(lax.axis_index("head") * channels, channels), channels)
        value = share[:, mine].astype(jnp.float32)
        for term in shared:
            value = value + term[...].astype(jnp.float32)
        out[:, first_half, :] = value.astype(out.dtype).reshape(shape)
        out[:, second_half, :] = second[rows:, :].reshape(shape)

    @pl.when(stage < last - 1)
    def _():
        out[:, second_half, :] = given[rows:, :].reshape(shape)

        @pl.when(stage % 2 == 0)
        def _():
            out[:, first_half, :] = shared[0][...].reshape(shape)

        @pl.when(stage % 2 == 1)
        def _():
            out[:, first_half, :] = given[:rows, :].reshape(shape)


def finish(last, row_count, total, second, given, share, shared):
    arrays = [total, second, given, share, *shared]
    return pl.pallas_call(
        functools.partial(finish_kernel, last),
        out_shape=jax.ShapeDtypeStruct((row_count, WIN, total.shape[1]), jnp.bfloat16),
        in_specs=[vmem] * len(arrays),
        out_specs=vmem,
        compiler_params=pltpu.CompilerParams(vmem_limit_bytes=VMEM_LIMIT),
        name="finish",
    )(*arrays)


def new_mark():
    return pl.pallas_call(
        lambda ref: None,
        out_shape=MARK,
        out_specs=anywhere,
        compiler_params=pltpu.CompilerParams(vmem_limit_bytes=1024 * 1024),
        name="new_mark",
    )()


def after(arrays, *marks, flops=0):
    shapes = tuple(jax.ShapeDtypeStruct(array.shape, array.dtype) for array in arrays)
    return pl.pallas_call(
        lambda *refs: None,
        out_shape=shapes,
        in_specs=[anywhere] * (len(arrays) + len(marks)),
        out_specs=(anywhere,) * len(arrays),
        input_output_aliases={place: place for place in range(len(arrays))},
        compiler_params=pltpu.CompilerParams(vmem_limit_bytes=1024 * 1024),
        cost_estimate=pl.CostEstimate(flops=flops, bytes_accessed=flops // 100, transcendentals=0),
        name="after",
    )(*arrays, *marks)


def per_device(stream, score_scale, value_weight, out_weight):
    row_count, col_count, width = stream.shape
    assert col_count == WIN, "one window"
    sections, n_win, n_head = (lax.axis_size(axis) for axis in AXES)
    assert sections % 2 == 0, "section pairs"
    value_cols, out_rows = value_weight[0], out_weight[0]
    places = [(win, group) for win in range(n_win) for group in range(n_head)]

    def send(value, start, stop, over=0, turn=0):
        return send_all(value, [(start, stop, over, turn)])

    def send_all(value, hops):
        at = lambda pipe, win, group: (pipe * n_win + win % n_win) * n_head + group % n_head
        pairs = [
            (at(start, win, group), at(stop, win + over, group + turn))
            for start, stop, over, turn in hops
            for win, group in places
        ]
        return lax.ppermute(value, AXES, pairs)

    piece = row_count * HALF
    natural = tuple(
        (chunk % 2) * row_count + chunk // 2 for chunk in range(row_count * col_count // HALF)
    )
    own = stream.reshape(row_count * col_count, width)
    arrived = [own] + [send(own, 0, 0, 0, turn) for turn in range(1, n_head)]
    mark = new_mark()
    blocks, filled = [], ()
    for turn, cells in enumerate(arrived):
        *block, mark = project(
            0, natural, [cells], mark, score_scale, value_cols, turn * own.shape[0], n_head * own.shape[0], filled
        )
        blocks.append(block)
        filled = block[2:]
    halves = [[(block, half * piece, piece) for block in range(n_head)] for half in range(2)]
    straight = tuple(range(row_count * n_head))
    kept = None

    for section in range(sections):
        shift = section % 2
        last = section + 1 == sections
        idle = (section + 2) % sections
        moved = []
        for half in range(2):
            share = section + 2 == sections and not half
            carried = [kept] if share or last and half else []
            if last and half:
                (mark,) = after([mark], given, *early)
            *part, mark = attend(section, halves[half], blocks, mark, out_rows, last, carried, share)
            if share:
                own_share, *shared = part
            cross = 0 if half else shift if last else 1 if shift else -1
            if last and half:
                terms = [send(part[turn], section, section - 1, 0, turn) for turn in range(1, n_head)]
                terms += [send(part[0], section, section - 1)]
            elif last:
                terms = [send(part[turn], section, section - 1, cross, turn) for turn in range(n_head)]
            elif shift and not half:
                terms = [send(part[0], section, idle, cross)]
            elif shift:
                terms = [send(part[0], section, section - 1, 0, turn) for turn in range(n_head)]
            else:
                terms = [send(part[0], section, section + 1, cross, turn) for turn in range(n_head)]
            moved.append(terms)
        if shift and not last:
            (one,) = after(moved[0], mark)
            moved[0] = [send(one, idle, section + 1, 0, turn) for turn in range(n_head)]
            total, mark = add(section - 1, moved[1], mark)
            moved[1] = [send(total, section - 1, section + 1)]
        if section + 2 == sections:
            straight_back = [(source, source - 1, 0, 0) for source in range(1, section + 1)]
            across = [(source, source - 1, 1, 0) for source in range(1, section, 2)]
            *shared, early_kept = after([*shared, kept], mark)
            early = [
                send_all(block, ([] if turn else across) + [(section, section, 0, turn + 1)])
                for turn, block in enumerate(shared)
            ]
            given = send_all(early_kept, straight_back)
            kept = None
        if not last:
            blocks, filled, rows = [], (), piece * n_head
            for half in range(2):
                keep_rows = 2 * rows if section + 2 < sections else half * rows
                *block, mark = project(
                    section + 1,
                    straight,
                    moved[half],
                    mark,
                    score_scale,
                    value_cols,
                    half * rows,
                    2 * rows,
                    filled,
                    kept,
                    keep_rows,
                )
                if keep_rows:
                    *block, kept = block
                blocks.append(block)
                filled = block[2:]
            halves = [[(0, 0, piece * n_head)], [(1, 0, piece * n_head)]]
    *across, mark = after([*moved[0][1:], mark], flops=4 * 10**9)
    first, mark = add(sections - 2, [moved[0][0], *across], mark, 10**8)
    second, mark = add(sections - 2, moved[1][:-1], mark, 4 * 10**9)
    total, mark = add(sections - 2, [second, moved[1][-1]], mark, 0, (first,))
    total = send(total, sections - 2, sections - 1)
    return finish(sections - 1, row_count * n_head, total, moved[1][-1], given, own_share, early)[None]


def solution(mesh):
    placed = (
        P("head", "win", None),
        P("pipe", None),
        P("pipe", None, "head"),
        P("pipe", "head", None),
    )
    return jax.shard_map(
        per_device,
        mesh=mesh,
        in_specs=placed,
        out_specs=P("pipe", None, "win", "head"),
        check_vma=False,
    )
```

```python
import functools
import math

import jax
import jax.numpy as jnp
from jax import lax
from jax.experimental import pallas as pl
from jax.experimental.pallas import tpu as pltpu
from jax.sharding import PartitionSpec as P

HEAD_DIM = 128
WIN = 32
HALF = WIN // 2
EPSILON = 1e-06
AXES = ("pipe", "win", "head")
VMEM_LIMIT = 14 * 1024 * 1024

vmem = pl.BlockSpec(memory_space=pltpu.VMEM)
anywhere = pl.BlockSpec(memory_space=pl.ANY)
MARK = jax.ShapeDtypeStruct((8, 128), jnp.float32)


def project_kernel(section, chunk_order, counts, n_filled, first_row, keep_row, mark, *refs):
    parts = []
    for count in counts:
        parts.append(refs[:count])
        refs = refs[count:]
    scale, weight = refs[:2]
    x_ref, q_ref, k_ref, v_ref, *kept, _ = refs[2 + n_filled :]
    channels = q_ref.shape[1]
    rows_here = len(chunk_order) * HALF

    @pl.when(lax.axis_index("pipe") == section)
    def _():
        mine = pl.ds(pl.multiple_of(lax.axis_index("head") * channels, channels), channels)
        inverse = [None] * len(chunk_order)
        for source, target in enumerate(chunk_order):
            rows = pl.ds(source * HALF, HALF)
            put = pl.ds(target * HALF, HALF)
            total = None
            for part in parts:
                term = join([columns[rows, :].astype(jnp.float32) for columns in part], 1)
                total = term if total is None else total + term
            x = total.astype(x_ref.dtype)
            x_ref[put, :] = x
            wide = x.astype(jnp.float32)
            mean_square = jnp.mean(wide * wide, axis=1, keepdims=True)
            inverse[target] = lax.rsqrt(mean_square + EPSILON)
        inverse = jnp.concatenate(inverse, axis=0)
        here = slice(first_row, first_row + rows_here)
        values = jnp.dot(x_ref[...], weight[...], preferred_element_type=jnp.float32)
        v_ref[here, :] = (values * inverse).astype(v_ref.dtype)
        key = (x_ref[:, mine].astype(jnp.float32) * inverse).astype(k_ref.dtype)
        k_ref[here, :] = key
        q_ref[...] = (key.astype(jnp.float32) * scale[:, mine]).astype(q_ref.dtype)
        for target in kept:
            target[keep_row : keep_row + rows_here, :] = x_ref[:, mine]


def project(section, chunk_order, parts, mark, scale, weight, first_row, total_rows, filled, kept=None, keep_rows=0):
    rows, (width, channels) = parts[0][0].shape[0], weight.shape
    shapes = [(rows, width), (rows, channels)] + [(total_rows, channels)] * 2
    shapes += [(keep_rows, channels)] if keep_rows else []
    counts = [len(part) for part in parts]
    arrays = [block for part in parts for block in part] + [scale, weight, *filled] + ([] if kept is None else [kept])
    at = 1 + sum(counts) + 2
    aliases = {at: 2, at + 1: 3} if filled else {}
    if kept is not None:
        aliases[len(arrays)] = 4
    keep_row = first_row if keep_rows > rows else 0
    return pl.pallas_call(
        functools.partial(
            project_kernel, section, chunk_order, counts, len(arrays) - at + 1, first_row, keep_row
        ),
        out_shape=tuple(jax.ShapeDtypeStruct(shape, jnp.bfloat16) for shape in shapes) + (MARK,),
        in_specs=[anywhere] + [vmem] * len(arrays),
        out_specs=(vmem,) * len(shapes) + (anywhere,),
        input_output_aliases=aliases,
        compiler_params=pltpu.CompilerParams(vmem_limit_bytes=VMEM_LIMIT),
        cost_estimate=pl.CostEstimate(
            flops=2 * rows * width * channels, bytes_accessed=2 * width * channels, transcendentals=0
        ),
        name="project",
    )(mark, *arrays)


def join(values, axis):
    return jnp.concatenate(values, axis=axis) if len(values) > 1 else values[0]


def attend_kernel(section, pieces, n_blocks, split, carry, copies, cut, mark, k, v, *refs):
    xs, qs, refs = refs[:n_blocks], refs[n_blocks : 2 * n_blocks], refs[2 * n_blocks :]
    weight, refs = refs[0], refs[1:]
    kept, refs = refs[:carry], refs[carry:]
    outs, o_ref = refs[:-2], refs[-1]
    channels = qs[0].shape[1]
    width = xs[0].shape[1]
    inv_root = 1.0 / math.sqrt(HEAD_DIM)
    n_head = width // channels

    @pl.when(lax.axis_index("pipe") == section)
    def _():
        heads = [slice(at, at + HEAD_DIM) for at in range(0, channels, HEAD_DIM)]
        ones = jnp.ones((v.shape[0], HEAD_DIM), jnp.bfloat16)
        weights = []
        for lanes in heads:
            q = join([qs[block][start : start + size, lanes] for block, start, size in pieces], 0)
            scores = lax.dot_general(
                q, k[:, lanes], (((1,), (1,)), ((), ())), preferred_element_type=jnp.float32
            )
            highest = jnp.max(scores, axis=1, keepdims=True)
            weights.append(jnp.exp((scores - highest) * inv_root).astype(jnp.bfloat16))
        for lanes, weight_of_head in zip(heads, weights):
            values = jnp.concatenate([v[:, lanes], ones], axis=1)
            attended = jnp.dot(weight_of_head, values, preferred_element_type=jnp.float32)
            o_ref[:, lanes] = (attended[:, :HEAD_DIM] / attended[:, HEAD_DIM:]).astype(o_ref.dtype)
        mine = jnp.where(lax.axis_index("head") == 0, 1.0, 0.0)
        attended = o_ref[...]
        step = channels if split else min(512, width)
        for column in range(0, width, step):
            if split:
                out = outs[column // step]
                block = lax.rem(lax.axis_index("head") + column // step, n_head)
                lanes = pl.ds(pl.multiple_of(block * step, step), step)
                put_lanes = slice(0, step)
            else:
                out = outs[0]
                lanes = put_lanes = slice(column, column + step)
                if cut:
                    part = column * 2 // width
                    cut_out, cut_lanes = outs[len(outs) - 2 + part], slice(column - part * width // 2, column - part * width // 2 + step)
            g = jnp.dot(attended, weight[:, lanes], preferred_element_type=jnp.float32)
            at = 0
            for turn, (block, start, size) in enumerate(pieces):
                residual = xs[block][start : start + size, lanes].astype(jnp.float32) * mine
                value = residual + g[at : at + size]
                if len(pieces) > 1:
                    place = lax.rem(lax.axis_index("head") + len(pieces) - turn, len(pieces)) * size
                    rows = pl.ds(pl.multiple_of(place, size), size)
                else:
                    rows = slice(0, size)
                value = value.astype(out.dtype)
                if len(outs) != 2 or not cut:
                    out[rows, put_lanes] = value
                if cut:
                    cut_out[rows, cut_lanes] = value
                at += size
        for turn in range(1, copies):
            block = lax.rem(lax.axis_index("head") + turn, n_head)
            lanes = pl.ds(pl.multiple_of(block * channels, channels), channels)
            outs[turn][...] = outs[0][:, lanes]

    if copies:

        @pl.when(lax.axis_index("pipe") != section)
        def _():
            outs[1][...] = kept[0][: o_ref.shape[0], :]

    elif carry:
        outs[0][o_ref.shape[0] :, :] = kept[0][...]


def attend(section, pieces, blocks, filled, mark, weight, split, kept=(), share=False, cut=False, whole=True):
    rows = sum(size for _, _, size in pieces)
    channels, width = weight.shape
    keys, values = filled
    n_head = width // channels
    if split:
        out_shape = tuple(
            jax.ShapeDtypeStruct((rows * (2 if kept and turn == 0 else 1), channels), jnp.bfloat16)
            for turn in range(n_head)
        )
    else:
        out_shape = (jax.ShapeDtypeStruct((rows, width), jnp.bfloat16),) * (1 if whole else 0)
        out_shape += (jax.ShapeDtypeStruct((rows, width // 2), jnp.bfloat16),) * (2 if cut else 0)
        out_shape += (jax.ShapeDtypeStruct((rows, channels), jnp.bfloat16),) * (n_head - 1 if share else 0)
    arrays = [keys, values] + [block[i] for i in range(2) for block in blocks] + [weight, *kept]
    return pl.pallas_call(
        functools.partial(attend_kernel, section, pieces, len(blocks), split, len(kept), n_head if share else 0, cut),
        out_shape=out_shape + (MARK,),
        in_specs=[anywhere] + [vmem] * len(arrays),
        out_specs=(vmem,) * len(out_shape) + (anywhere,),
        scratch_shapes=[pltpu.VMEM((rows, channels), jnp.bfloat16)],
        compiler_params=pltpu.CompilerParams(vmem_limit_bytes=VMEM_LIMIT),
        cost_estimate=pl.CostEstimate(
            flops=2 * rows * channels * (width + 2 * keys.shape[0]),
            bytes_accessed=2 * width * channels,
            transcendentals=rows * keys.shape[0] * channels // HEAD_DIM,
        ),
        name="attend",
    )(mark, *arrays)


def add_kernel(section, n_before, number, mark, *refs):
    @pl.when(lax.axis_index("pipe") == section)
    def _():
        before, terms, out = refs[:n_before], refs[n_before:-2], refs[-2]
        rows = out.shape[0] - sum(block.shape[0] for block in before)
        width = out.shape[1]
        lanes = [slice(0, width) if term.shape[1] == width else slice(number * width, (number + 1) * width) for term in terms]
        total = terms[0][:rows, lanes[0]].astype(jnp.float32)
        for term, columns in zip(terms[1:], lanes[1:]):
            total = total + term[:rows, columns].astype(jnp.float32)
        for block in before:
            out[: block.shape[0], :] = block[...]
        out[out.shape[0] - rows :, :] = total.astype(out.dtype)


def add(section, terms, mark, flops=0, before=(), number=0):
    rows, width = min(term.shape for term in terms)
    rows += sum(block.shape[0] for block in before)
    return pl.pallas_call(
        functools.partial(add_kernel, section, len(before), number),
        out_shape=(jax.ShapeDtypeStruct((rows, width), terms[0].dtype), MARK),
        in_specs=[anywhere] + [vmem] * (len(before) + len(terms)),
        out_specs=(vmem, anywhere),
        compiler_params=pltpu.CompilerParams(vmem_limit_bytes=VMEM_LIMIT),
        cost_estimate=pl.CostEstimate(flops=flops, bytes_accessed=flops // 100, transcendentals=0),
        name="add",
    )(mark, *before, *terms)


def finish_kernel(last, total, second, given, share, *refs):
    shared, out = refs[:-1], refs[-1]
    shape = (out.shape[0], HALF, out.shape[2])
    rows, channels = shared[0].shape
    stage = lax.axis_index("pipe")
    first_half, second_half = (slice(half * HALF, (half + 1) * HALF) for half in range(2))

    @pl.when(stage == last)
    def _():
        out[:, first_half, :] = total[:rows, :].reshape(shape)
        out[:, second_half, :] = total[rows:, :].reshape(shape)

    @pl.when(stage == last - 1)
    def _():
        mine = pl.ds(pl.multiple_of(lax.axis_index("head") * channels, channels), channels)
        value = share[:, mine].astype(jnp.float32)
        for term in shared:
            value = value + term[...].astype(jnp.float32)
        out[:, first_half, :] = value.astype(out.dtype).reshape(shape)
        out[:, second_half, :] = second[rows:, :].reshape(shape)

    @pl.when(stage < last - 1)
    def _():
        out[:, second_half, :] = given[rows:, :].reshape(shape)

        @pl.when(stage % 2 == 0)
        def _():
            out[:, first_half, :] = shared[0][...].reshape(shape)

        @pl.when(stage % 2 == 1)
        def _():
            out[:, first_half, :] = given[:rows, :].reshape(shape)


def finish(last, row_count, total, second, given, share, shared):
    arrays = [total, second, given, share, *shared]
    return pl.pallas_call(
        functools.partial(finish_kernel, last),
        out_shape=jax.ShapeDtypeStruct((row_count, WIN, total.shape[1]), jnp.bfloat16),
        in_specs=[vmem] * len(arrays),
        out_specs=vmem,
        compiler_params=pltpu.CompilerParams(vmem_limit_bytes=VMEM_LIMIT),
        name="finish",
    )(*arrays)


def new_mark():
    return pl.pallas_call(
        lambda ref: None,
        out_shape=MARK,
        out_specs=anywhere,
        compiler_params=pltpu.CompilerParams(vmem_limit_bytes=1024 * 1024),
        name="new_mark",
    )()


def after(arrays, *marks, flops=0):
    shapes = tuple(jax.ShapeDtypeStruct(array.shape, array.dtype) for array in arrays)
    return pl.pallas_call(
        lambda *refs: None,
        out_shape=shapes,
        in_specs=[anywhere] * (len(arrays) + len(marks)),
        out_specs=(anywhere,) * len(arrays),
        input_output_aliases={place: place for place in range(len(arrays))},
        compiler_params=pltpu.CompilerParams(vmem_limit_bytes=1024 * 1024),
        cost_estimate=pl.CostEstimate(flops=flops, bytes_accessed=flops // 100, transcendentals=0),
        name="after",
    )(*arrays, *marks)


def per_device(stream, score_scale, value_weight, out_weight):
    row_count, col_count, width = stream.shape
    assert col_count == WIN, "one window"
    sections, n_win, n_head = (lax.axis_size(axis) for axis in AXES)
    assert sections % 2 == 0, "section pairs"
    value_cols, out_rows = value_weight[0], out_weight[0]
    places = [(win, group) for win in range(n_win) for group in range(n_head)]

    def send(value, start, stop, over=0, turn=0):
        return send_all(value, [(start, stop, over, turn)])

    def send_all(value, hops):
        at = lambda pipe, win, group: (pipe * n_win + win % n_win) * n_head + group % n_head
        pairs = [
            (at(start, win, group), at(stop, win + over, group + turn))
            for start, stop, over, turn in hops
            for win, group in places
        ]
        return lax.ppermute(value, AXES, pairs)

    piece = row_count * HALF
    natural = tuple(
        (chunk % 2) * row_count + chunk // 2 for chunk in range(row_count * col_count // HALF)
    )
    own = stream.reshape(row_count * col_count, width)
    arrived = [own] + [send(own, 0, 0, 0, turn) for turn in range(1, n_head)]
    mark = new_mark()
    blocks, filled = [], ()
    for turn, cells in enumerate(arrived):
        *block, mark = project(
            0, natural, [[cells]], mark, score_scale, value_cols, turn * own.shape[0], n_head * own.shape[0], filled
        )
        blocks.append(block)
        filled = block[2:]
    halves = [[(block, half * piece, piece) for block in range(n_head)] for half in range(2)]
    straight = tuple(range(row_count * n_head))
    kept = None

    for section in range(sections):
        shift = section % 2
        last = section + 1 == sections
        idle = (section + 2) % sections
        moved = []
        for half in range(2):
            share = section + 2 == sections and not half
            carried = [kept] if share or last and half else []
            if last and half:
                (mark,) = after([mark], given, *early)
            cut = shift == 1 and half == 1 and not last
            whole = not cut
            *part, mark = attend(
                section, halves[half], blocks, filled, mark, out_rows, last, carried, share, cut, whole
            )
            if share:
                own_share, *shared = part
            cross = 0 if half else shift if last else 1 if shift else -1
            if last and half:
                terms = [send(part[turn], section, section - 1, 0, turn) for turn in range(1, n_head)]
                terms += [send(part[0], section, section - 1)]
            elif last:
                terms = [send(part[turn], section, section - 1, cross, turn) for turn in range(n_head)]
            elif shift and not half:
                terms = [send(block, section, idle, cross) for block in part]
            elif shift:
                terms = [[send(block, section, section - 1, 0, turn) for turn in range(n_head)] for block in part]
            else:
                terms = [[send(part[0], section, section + 1, cross, turn)] for turn in range(n_head)]
            moved.append(terms)
        if shift and not last:
            arrived = [after([block], mark, flops=0)[0] for block in moved[0]]
            moved[0] = [
                [send(block, idle, section + 1, 0, turn) for block in arrived] for turn in range(n_head)
            ]
            sums = []
            for number, terms in enumerate(moved[1]):
                total, mark = add(section - 1, terms, mark, 0)
                sums.append(send(total, section - 1, section + 1))
            moved[1] = [sums]
        if section + 2 == sections:
            straight_back = [(source, source - 1, 0, 0) for source in range(1, section + 1)]
            across = [(source, source - 1, 1, 0) for source in range(1, section, 2)]
            *shared, early_kept = after([*shared, kept], mark)
            early = [
                send_all(block, ([] if turn else across) + [(section, section, 0, turn + 1)])
                for turn, block in enumerate(shared)
            ]
            given = send_all(early_kept, straight_back)
            kept = None
        if not last:
            blocks, filled, rows = [None, None], (), piece * n_head
            for half in (1, 0) if shift else (0, 1):
                keep_rows = 2 * rows if section + 2 < sections else half * rows
                *block, mark = project(
                    section + 1,
                    straight,
                    moved[half],
                    mark,
                    score_scale,
                    value_cols,
                    half * rows,
                    2 * rows,
                    filled,
                    kept,
                    keep_rows,
                )
                if keep_rows:
                    *block, kept = block
                blocks[half] = block
                filled = block[2:]
            halves = [[(0, 0, piece * n_head)], [(1, 0, piece * n_head)]]
    *across, mark = after([*moved[0][1:], mark], flops=4 * 10**9)
    first, mark = add(sections - 2, [moved[0][0], *across], mark, 10**8)
    second, mark = add(sections - 2, moved[1][:-1], mark, 4 * 10**9)
    total, mark = add(sections - 2, [second, moved[1][-1]], mark, 0, (first,))
    total = send(total, sections - 2, sections - 1)
    return finish(sections - 1, row_count * n_head, total, moved[1][-1], given, own_share, early)[None]


def solution(mesh):
    placed = (
        P("head", "win", None),
        P("pipe", None),
        P("pipe", None, "head"),
        P("pipe", "head", None),
    )
    return jax.shard_map(
        per_device,
        mesh=mesh,
        in_specs=placed,
        out_specs=P("pipe", None, "win", "head"),
        check_vma=False,
    )
```

```python
import functools
import math

import jax
import jax.numpy as jnp
from jax import lax
from jax.experimental import pallas as pl
from jax.experimental.pallas import tpu as pltpu
from jax.sharding import PartitionSpec as P

HEAD_DIM = 128
WIN = 32
HALF = WIN // 2
EPSILON = 1e-06
AXES = ("pipe", "win", "head")
VMEM_LIMIT = 14 * 1024 * 1024

vmem = pl.BlockSpec(memory_space=pltpu.VMEM)
anywhere = pl.BlockSpec(memory_space=pl.ANY)
MARK = jax.ShapeDtypeStruct((8, 128), jnp.float32)


def project_kernel(section, chunk_order, counts, n_filled, first_row, keep_row, mark, *refs):
    parts = []
    for count in counts:
        parts.append(refs[:count])
        refs = refs[count:]
    scale, weight = refs[:2]
    x_ref, q_ref, k_ref, v_ref, *kept, _ = refs[2 + n_filled :]
    channels = q_ref.shape[1]
    rows_here = len(chunk_order) * HALF

    @pl.when(lax.axis_index("pipe") == section)
    def _():
        mine = pl.ds(pl.multiple_of(lax.axis_index("head") * channels, channels), channels)
        inverse = [None] * len(chunk_order)
        for source, target in enumerate(chunk_order):
            rows = pl.ds(source * HALF, HALF)
            put = pl.ds(target * HALF, HALF)
            total = None
            for part in parts:
                term = join([columns[rows, :].astype(jnp.float32) for columns in part], 1)
                total = term if total is None else total + term
            x = total.astype(x_ref.dtype)
            x_ref[put, :] = x
            wide = x.astype(jnp.float32)
            mean_square = jnp.mean(wide * wide, axis=1, keepdims=True)
            inverse[target] = lax.rsqrt(mean_square + EPSILON)
        inverse = jnp.concatenate(inverse, axis=0)
        here = slice(first_row, first_row + rows_here)
        values = jnp.dot(x_ref[...], weight[...], preferred_element_type=jnp.float32)
        v_ref[here, :] = (values * inverse).astype(v_ref.dtype)
        key = (x_ref[:, mine].astype(jnp.float32) * inverse).astype(k_ref.dtype)
        k_ref[here, :] = key
        q_ref[...] = (key.astype(jnp.float32) * scale[:, mine]).astype(q_ref.dtype)
        for target in kept:
            target[keep_row : keep_row + rows_here, :] = x_ref[:, mine]


def project(section, chunk_order, parts, mark, scale, weight, first_row, total_rows, filled, kept=None, keep_rows=0):
    rows, (width, channels) = parts[0][0].shape[0], weight.shape
    shapes = [(rows, width), (rows, channels)] + [(total_rows, channels)] * 2
    shapes += [(keep_rows, channels)] if keep_rows else []
    counts = [len(part) for part in parts]
    arrays = [block for part in parts for block in part] + [scale, weight, *filled] + ([] if kept is None else [kept])
    at = 1 + sum(counts) + 2
    aliases = {at: 2, at + 1: 3} if filled else {}
    if kept is not None:
        aliases[len(arrays)] = 4
    keep_row = first_row if keep_rows > rows else 0
    return pl.pallas_call(
        functools.partial(
            project_kernel, section, chunk_order, counts, len(arrays) - at + 1, first_row, keep_row
        ),
        out_shape=tuple(jax.ShapeDtypeStruct(shape, jnp.bfloat16) for shape in shapes) + (MARK,),
        in_specs=[anywhere] + [vmem] * len(arrays),
        out_specs=(vmem,) * len(shapes) + (anywhere,),
        input_output_aliases=aliases,
        compiler_params=pltpu.CompilerParams(vmem_limit_bytes=VMEM_LIMIT),
        cost_estimate=pl.CostEstimate(
            flops=2 * rows * width * channels, bytes_accessed=2 * width * channels, transcendentals=0
        ),
        name="project",
    )(mark, *arrays)


def join(values, axis):
    return jnp.concatenate(values, axis=axis) if len(values) > 1 else values[0]


def attend_kernel(section, pieces, n_blocks, split, carry, copies, cut, mark, k, v, *refs):
    xs, qs, refs = refs[:n_blocks], refs[n_blocks : 2 * n_blocks], refs[2 * n_blocks :]
    weight, refs = refs[0], refs[1:]
    kept, refs = refs[:carry], refs[carry:]
    outs, o_ref = refs[:-2], refs[-1]
    channels = qs[0].shape[1]
    width = xs[0].shape[1]
    inv_root = 1.0 / math.sqrt(HEAD_DIM)
    n_head = width // channels

    @pl.when(lax.axis_index("pipe") == section)
    def _():
        heads = [slice(at, at + HEAD_DIM) for at in range(0, channels, HEAD_DIM)]
        ones = jnp.ones((v.shape[0], HEAD_DIM), jnp.bfloat16)
        weights = []
        for lanes in heads:
            q = join([qs[block][start : start + size, lanes] for block, start, size in pieces], 0)
            scores = lax.dot_general(
                q, k[:, lanes], (((1,), (1,)), ((), ())), preferred_element_type=jnp.float32
            )
            highest = jnp.max(scores, axis=1, keepdims=True)
            weights.append(jnp.exp((scores - highest) * inv_root).astype(jnp.bfloat16))
        for lanes, weight_of_head in zip(heads, weights):
            values = jnp.concatenate([v[:, lanes], ones], axis=1)
            attended = jnp.dot(weight_of_head, values, preferred_element_type=jnp.float32)
            o_ref[:, lanes] = (attended[:, :HEAD_DIM] / attended[:, HEAD_DIM:]).astype(o_ref.dtype)
        mine = jnp.where(lax.axis_index("head") == 0, 1.0, 0.0)
        attended = o_ref[...]
        step = channels if split else min(512, width)
        for column in range(0, width, step):
            if split:
                out = outs[column // step]
                block = lax.rem(lax.axis_index("head") + column // step, n_head)
                lanes = pl.ds(pl.multiple_of(block * step, step), step)
                put_lanes = slice(0, step)
            else:
                out = outs[0]
                lanes = put_lanes = slice(column, column + step)
                if cut:
                    part = column * 2 // width
                    cut_out, cut_lanes = outs[len(outs) - 2 + part], slice(column - part * width // 2, column - part * width // 2 + step)
            g = jnp.dot(attended, weight[:, lanes], preferred_element_type=jnp.float32)
            at = 0
            for turn, (block, start, size) in enumerate(pieces):
                residual = xs[block][start : start + size, lanes].astype(jnp.float32) * mine
                value = residual + g[at : at + size]
                if len(pieces) > 1:
                    place = lax.rem(lax.axis_index("head") + len(pieces) - turn, len(pieces)) * size
                    rows = pl.ds(pl.multiple_of(place, size), size)
                else:
                    rows = slice(0, size)
                value = value.astype(out.dtype)
                if len(outs) != 2 or not cut:
                    out[rows, put_lanes] = value
                if cut:
                    cut_out[rows, cut_lanes] = value
                at += size
        for turn in range(1, copies):
            block = lax.rem(lax.axis_index("head") + turn, n_head)
            lanes = pl.ds(pl.multiple_of(block * channels, channels), channels)
            outs[turn][...] = outs[0][:, lanes]

    if copies:

        @pl.when(lax.axis_index("pipe") != section)
        def _():
            outs[1][...] = kept[0][: o_ref.shape[0], :]

    elif carry:
        outs[0][o_ref.shape[0] :, :] = kept[0][...]


def attend(section, pieces, blocks, filled, mark, weight, split, kept=(), share=False, cut=False, whole=True):
    rows = sum(size for _, _, size in pieces)
    channels, width = weight.shape
    keys, values = filled
    n_head = width // channels
    if split:
        out_shape = tuple(
            jax.ShapeDtypeStruct((rows * (2 if kept and turn == 0 else 1), channels), jnp.bfloat16)
            for turn in range(n_head)
        )
    else:
        out_shape = (jax.ShapeDtypeStruct((rows, width), jnp.bfloat16),) * (1 if whole else 0)
        out_shape += (jax.ShapeDtypeStruct((rows, width // 2), jnp.bfloat16),) * (2 if cut else 0)
        out_shape += (jax.ShapeDtypeStruct((rows, channels), jnp.bfloat16),) * (n_head - 1 if share else 0)
    arrays = [keys, values] + [block[i] for i in range(2) for block in blocks] + [weight, *kept]
    return pl.pallas_call(
        functools.partial(attend_kernel, section, pieces, len(blocks), split, len(kept), n_head if share else 0, cut),
        out_shape=out_shape + (MARK,),
        in_specs=[anywhere] + [vmem] * len(arrays),
        out_specs=(vmem,) * len(out_shape) + (anywhere,),
        scratch_shapes=[pltpu.VMEM((rows, channels), jnp.bfloat16)],
        compiler_params=pltpu.CompilerParams(vmem_limit_bytes=VMEM_LIMIT),
        cost_estimate=pl.CostEstimate(
            flops=2 * rows * channels * (width + 2 * keys.shape[0]),
            bytes_accessed=2 * width * channels,
            transcendentals=rows * keys.shape[0] * channels // HEAD_DIM,
        ),
        name="attend",
    )(mark, *arrays)


def add_kernel(section, n_before, number, mark, *refs):
    @pl.when(lax.axis_index("pipe") == section)
    def _():
        before, terms, out = refs[:n_before], refs[n_before:-2], refs[-2]
        rows = out.shape[0] - sum(block.shape[0] for block in before)
        width = out.shape[1]
        lanes = [slice(0, width) if term.shape[1] == width else slice(number * width, (number + 1) * width) for term in terms]
        total = terms[0][:rows, lanes[0]].astype(jnp.float32)
        for term, columns in zip(terms[1:], lanes[1:]):
            total = total + term[:rows, columns].astype(jnp.float32)
        for block in before:
            out[: block.shape[0], :] = block[...]
        out[out.shape[0] - rows :, :] = total.astype(out.dtype)


def add(section, terms, mark, flops=0, before=(), number=0):
    rows, width = min(term.shape for term in terms)
    rows += sum(block.shape[0] for block in before)
    return pl.pallas_call(
        functools.partial(add_kernel, section, len(before), number),
        out_shape=(jax.ShapeDtypeStruct((rows, width), terms[0].dtype), MARK),
        in_specs=[anywhere] + [vmem] * (len(before) + len(terms)),
        out_specs=(vmem, anywhere),
        compiler_params=pltpu.CompilerParams(vmem_limit_bytes=VMEM_LIMIT),
        cost_estimate=pl.CostEstimate(flops=flops, bytes_accessed=flops // 100, transcendentals=0),
        name="add",
    )(mark, *before, *terms)


def finish_kernel(last, total, second, given, share, *refs):
    shared, out = refs[:-1], refs[-1]
    shape = (out.shape[0], HALF, out.shape[2])
    rows, channels = shared[0].shape
    stage = lax.axis_index("pipe")
    first_half, second_half = (slice(half * HALF, (half + 1) * HALF) for half in range(2))

    @pl.when(stage == last)
    def _():
        out[:, first_half, :] = total[:rows, :].reshape(shape)
        out[:, second_half, :] = total[rows:, :].reshape(shape)

    @pl.when(stage == last - 1)
    def _():
        mine = pl.ds(pl.multiple_of(lax.axis_index("head") * channels, channels), channels)
        value = share[:, mine].astype(jnp.float32)
        for term in shared:
            value = value + term[...].astype(jnp.float32)
        out[:, first_half, :] = value.astype(out.dtype).reshape(shape)
        out[:, second_half, :] = second[rows:, :].reshape(shape)

    @pl.when(stage < last - 1)
    def _():
        out[:, second_half, :] = given[rows:, :].reshape(shape)

        @pl.when(stage % 2 == 0)
        def _():
            out[:, first_half, :] = shared[0][...].reshape(shape)

        @pl.when(stage % 2 == 1)
        def _():
            out[:, first_half, :] = given[:rows, :].reshape(shape)


def finish(last, row_count, total, second, given, share, shared):
    arrays = [total, second, given, share, *shared]
    return pl.pallas_call(
        functools.partial(finish_kernel, last),
        out_shape=jax.ShapeDtypeStruct((row_count, WIN, total.shape[1]), jnp.bfloat16),
        in_specs=[vmem] * len(arrays),
        out_specs=vmem,
        compiler_params=pltpu.CompilerParams(vmem_limit_bytes=VMEM_LIMIT),
        name="finish",
    )(*arrays)


def new_mark():
    return pl.pallas_call(
        lambda ref: None,
        out_shape=MARK,
        out_specs=anywhere,
        compiler_params=pltpu.CompilerParams(vmem_limit_bytes=1024 * 1024),
        name="new_mark",
    )()


def after(arrays, *marks, flops=0):
    shapes = tuple(jax.ShapeDtypeStruct(array.shape, array.dtype) for array in arrays)
    return pl.pallas_call(
        lambda *refs: None,
        out_shape=shapes,
        in_specs=[anywhere] * (len(arrays) + len(marks)),
        out_specs=(anywhere,) * len(arrays),
        input_output_aliases={place: place for place in range(len(arrays))},
        compiler_params=pltpu.CompilerParams(vmem_limit_bytes=1024 * 1024),
        cost_estimate=pl.CostEstimate(flops=flops, bytes_accessed=flops // 100, transcendentals=0),
        name="after",
    )(*arrays, *marks)


def per_device(stream, score_scale, value_weight, out_weight):
    row_count, col_count, width = stream.shape
    assert col_count == WIN, "one window"
    sections, n_win, n_head = (lax.axis_size(axis) for axis in AXES)
    assert sections % 2 == 0, "section pairs"
    value_cols, out_rows = value_weight[0], out_weight[0]
    places = [(win, group) for win in range(n_win) for group in range(n_head)]

    def send(value, start, stop, over=0, turn=0):
        return send_all(value, [(start, stop, over, turn)])

    def send_all(value, hops):
        at = lambda pipe, win, group: (pipe * n_win + win % n_win) * n_head + group % n_head
        pairs = [
            (at(start, win, group), at(stop, win + over, group + turn))
            for start, stop, over, turn in hops
            for win, group in places
        ]
        return lax.ppermute(value, AXES, pairs)

    piece = row_count * HALF
    natural = tuple(
        (chunk % 2) * row_count + chunk // 2 for chunk in range(row_count * col_count // HALF)
    )
    own = stream.reshape(row_count * col_count, width)
    arrived = [own] + [send(own, 0, 0, 0, turn) for turn in range(1, n_head)]
    mark = new_mark()
    blocks, filled = [], ()
    for turn, cells in enumerate(arrived):
        *block, mark = project(
            0, natural, [[cells]], mark, score_scale, value_cols, turn * own.shape[0], n_head * own.shape[0], filled
        )
        blocks.append(block)
        filled = block[2:]
    halves = [[(block, half * piece, piece) for block in range(n_head)] for half in range(2)]
    straight = tuple(range(row_count * n_head))
    kept = None

    for section in range(sections):
        shift = section % 2
        last = section + 1 == sections
        idle = (section + 2) % sections
        moved = []
        for half in range(2):
            share = section + 2 == sections and not half
            carried = [kept] if share or last and half else []
            if last and half:
                (mark,) = after([mark], given, *early)
            cut = shift == 1 and half == 1 and not last
            whole = not cut
            *part, mark = attend(
                section, halves[half], blocks, filled, mark, out_rows, last, carried, share, cut, whole
            )
            if share:
                own_share, *shared = part
            cross = 0 if half else shift if last else 1 if shift else -1
            if last and half:
                terms = [send(part[turn], section, section - 1, 0, turn) for turn in range(1, n_head)]
                terms += [send(part[0], section, section - 1)]
            elif last:
                terms = [send(part[turn], section, section - 1, cross, turn) for turn in range(n_head)]
            elif shift and not half:
                terms = [send(block, section, idle, cross) for block in part]
            elif shift:
                terms = [[send(block, section, section - 1, 0, turn) for turn in range(n_head)] for block in part]
            else:
                terms = [[send(part[0], section, section + 1, cross, turn)] for turn in range(n_head)]
            moved.append(terms)
        if shift and not last:
            arrived = [after([block], mark, flops=0)[0] for block in moved[0]]
            moved[0] = [
                [send(block, idle, section + 1, 0, turn) for block in arrived] for turn in range(n_head)
            ]
            sums = []
            for number, terms in enumerate(moved[1]):
                total, mark = add(section - 1, terms, mark, 0)
                sums.append(send(total, section - 1, section + 1))
            moved[1] = [sums]
        if section + 2 == sections:
            straight_back = [(source, source - 1, 0, 0) for source in range(1, section + 1)]
            across = [(source, source - 1, 1, 0) for source in range(1, section, 2)]
            *shared, early_kept = after([*shared, kept], mark)
            early = [
                send_all(block, ([] if turn else across) + [(section, section, 0, turn + 1)])
                for turn, block in enumerate(shared)
            ]
            given = send_all(early_kept, straight_back)
            kept = None
        if not last:
            blocks, filled, rows = [None, None], (), piece * n_head
            for half in (1, 0) if shift else (0, 1):
                keep_rows = 2 * rows if section + 2 < sections else half * rows
                *block, mark = project(
                    section + 1,
                    straight,
                    moved[half],
                    mark,
                    score_scale,
                    value_cols,
                    half * rows,
                    2 * rows,
                    filled,
                    kept,
                    keep_rows,
                )
                if keep_rows:
                    *block, kept = block
                blocks[half] = block
                filled = block[2:]
            halves = [[(0, 0, piece * n_head)], [(1, 0, piece * n_head)]]
    *across, mark = after([*moved[0][1:], mark])
    first, mark = add(sections - 2, [moved[0][0], *across], mark, 4 * 10**9)
    second, mark = add(sections - 2, moved[1][:-1], mark, 4 * 10**9)
    total, mark = add(sections - 2, [second, moved[1][-1]], mark, 0, (first,))
    total = send(total, sections - 2, sections - 1)
    return finish(sections - 1, row_count * n_head, total, moved[1][-1], given, own_share, early)[None]


def solution(mesh):
    placed = (
        P("head", "win", None),
        P("pipe", None),
        P("pipe", None, "head"),
        P("pipe", "head", None),
    )
    return jax.shard_map(
        per_device,
        mesh=mesh,
        in_specs=placed,
        out_specs=P("pipe", None, "win", "head"),
        check_vma=False,
    )
```

```python
import functools
import math

import jax
import jax.numpy as jnp
from jax import lax
from jax.experimental import pallas as pl
from jax.experimental.pallas import tpu as pltpu
from jax.sharding import PartitionSpec as P

HEAD_DIM = 128
WIN = 32
HALF = WIN // 2
EPSILON = 1e-06
AXES = ("pipe", "win", "head")
VMEM_LIMIT = 14 * 1024 * 1024

vmem = pl.BlockSpec(memory_space=pltpu.VMEM)
anywhere = pl.BlockSpec(memory_space=pl.ANY)
MARK = jax.ShapeDtypeStruct((8, 128), jnp.float32)


def project_kernel(section, chunk_order, counts, n_filled, first_row, keep_row, mark, *refs):
    parts = []
    for count in counts:
        parts.append(refs[:count])
        refs = refs[count:]
    scale, weight = refs[:2]
    x_ref, q_ref, k_ref, v_ref, *kept, _ = refs[2 + n_filled :]
    channels = q_ref.shape[1]
    rows_here = len(chunk_order) * HALF

    @pl.when(lax.axis_index("pipe") == section)
    def _():
        mine = pl.ds(pl.multiple_of(lax.axis_index("head") * channels, channels), channels)
        inverse = [None] * len(chunk_order)
        for source, target in enumerate(chunk_order):
            rows = pl.ds(source * HALF, HALF)
            put = pl.ds(target * HALF, HALF)
            total = None
            for part in parts:
                term = join([columns[rows, :].astype(jnp.float32) for columns in part], 1)
                total = term if total is None else total + term
            x = total.astype(x_ref.dtype)
            x_ref[put, :] = x
            wide = x.astype(jnp.float32)
            mean_square = jnp.mean(wide * wide, axis=1, keepdims=True)
            inverse[target] = lax.rsqrt(mean_square + EPSILON)
        inverse = jnp.concatenate(inverse, axis=0)
        here = slice(first_row, first_row + rows_here)
        values = jnp.dot(x_ref[...], weight[...], preferred_element_type=jnp.float32)
        v_ref[here, :] = (values * inverse).astype(v_ref.dtype)
        key = (x_ref[:, mine].astype(jnp.float32) * inverse).astype(k_ref.dtype)
        k_ref[here, :] = key
        q_ref[...] = (key.astype(jnp.float32) * scale[:, mine]).astype(q_ref.dtype)
        for target in kept:
            target[keep_row : keep_row + rows_here, :] = x_ref[:, mine]


def project(section, chunk_order, parts, mark, scale, weight, first_row, total_rows, filled, kept=None, keep_rows=0):
    rows, (width, channels) = parts[0][0].shape[0], weight.shape
    shapes = [(rows, width), (rows, channels)] + [(total_rows, channels)] * 2
    shapes += [(keep_rows, channels)] if keep_rows else []
    counts = [len(part) for part in parts]
    arrays = [block for part in parts for block in part] + [scale, weight, *filled] + ([] if kept is None else [kept])
    at = 1 + sum(counts) + 2
    aliases = {at: 2, at + 1: 3} if filled else {}
    if kept is not None:
        aliases[len(arrays)] = 4
    keep_row = first_row if keep_rows > rows else 0
    return pl.pallas_call(
        functools.partial(
            project_kernel, section, chunk_order, counts, len(arrays) - at + 1, first_row, keep_row
        ),
        out_shape=tuple(jax.ShapeDtypeStruct(shape, jnp.bfloat16) for shape in shapes) + (MARK,),
        in_specs=[anywhere] + [vmem] * len(arrays),
        out_specs=(vmem,) * len(shapes) + (anywhere,),
        input_output_aliases=aliases,
        compiler_params=pltpu.CompilerParams(vmem_limit_bytes=VMEM_LIMIT),
        cost_estimate=pl.CostEstimate(
            flops=2 * rows * width * channels, bytes_accessed=2 * width * channels, transcendentals=0
        ),
        name="project",
    )(mark, *arrays)


def join(values, axis):
    return jnp.concatenate(values, axis=axis) if len(values) > 1 else values[0]


def attend_kernel(section, pieces, n_blocks, split, carry, copies, cut, mark, k, v, *refs):
    xs, qs, refs = refs[:n_blocks], refs[n_blocks : 2 * n_blocks], refs[2 * n_blocks :]
    weight, refs = refs[0], refs[1:]
    kept, refs = refs[:carry], refs[carry:]
    outs, o_ref = refs[:-2], refs[-1]
    channels = qs[0].shape[1]
    width = xs[0].shape[1]
    inv_root = 1.0 / math.sqrt(HEAD_DIM)
    n_head = width // channels

    @pl.when(lax.axis_index("pipe") == section)
    def _():
        heads = [slice(at, at + HEAD_DIM) for at in range(0, channels, HEAD_DIM)]
        ones = jnp.ones((v.shape[0], HEAD_DIM), jnp.bfloat16)
        weights = []
        for lanes in heads:
            q = join([qs[block][start : start + size, lanes] for block, start, size in pieces], 0)
            scores = lax.dot_general(
                q, k[:, lanes], (((1,), (1,)), ((), ())), preferred_element_type=jnp.float32
            )
            highest = jnp.max(scores, axis=1, keepdims=True)
            weights.append(jnp.exp((scores - highest) * inv_root).astype(jnp.bfloat16))
        for lanes, weight_of_head in zip(heads, weights):
            values = jnp.concatenate([v[:, lanes], ones], axis=1)
            attended = jnp.dot(weight_of_head, values, preferred_element_type=jnp.float32)
            o_ref[:, lanes] = (attended[:, :HEAD_DIM] / attended[:, HEAD_DIM:]).astype(o_ref.dtype)
        mine = jnp.where(lax.axis_index("head") == 0, 1.0, 0.0)
        attended = o_ref[...]
        step = channels if split else min(512, width)
        for column in range(0, width, step):
            if split:
                out = outs[column // step]
                block = lax.rem(lax.axis_index("head") + column // step, n_head)
                lanes = pl.ds(pl.multiple_of(block * step, step), step)
                put_lanes = slice(0, step)
            else:
                out = outs[0]
                lanes = put_lanes = slice(column, column + step)
                if cut:
                    part = column * 2 // width
                    cut_out, cut_lanes = outs[len(outs) - 2 + part], slice(column - part * width // 2, column - part * width // 2 + step)
            g = jnp.dot(attended, weight[:, lanes], preferred_element_type=jnp.float32)
            at = 0
            for turn, (block, start, size) in enumerate(pieces):
                residual = xs[block][start : start + size, lanes].astype(jnp.float32) * mine
                value = residual + g[at : at + size]
                if len(pieces) > 1:
                    place = lax.rem(lax.axis_index("head") + len(pieces) - turn, len(pieces)) * size
                    rows = pl.ds(pl.multiple_of(place, size), size)
                else:
                    rows = slice(0, size)
                value = value.astype(out.dtype)
                if len(outs) != 2 or not cut:
                    out[rows, put_lanes] = value
                if cut:
                    cut_out[rows, cut_lanes] = value
                at += size
        for turn in range(1, copies):
            block = lax.rem(lax.axis_index("head") + turn, n_head)
            lanes = pl.ds(pl.multiple_of(block * channels, channels), channels)
            outs[turn][...] = outs[0][:, lanes]

    if copies:

        @pl.when(lax.axis_index("pipe") != section)
        def _():
            outs[1][...] = kept[0][: o_ref.shape[0], :]

    elif carry:
        outs[0][o_ref.shape[0] :, :] = kept[0][...]


def attend(section, pieces, blocks, filled, mark, weight, split, kept=(), share=False, cut=False, whole=True):
    rows = sum(size for _, _, size in pieces)
    channels, width = weight.shape
    keys, values = filled
    n_head = width // channels
    if split:
        out_shape = tuple(
            jax.ShapeDtypeStruct((rows * (2 if kept and turn == 0 else 1), channels), jnp.bfloat16)
            for turn in range(n_head)
        )
    else:
        out_shape = (jax.ShapeDtypeStruct((rows, width), jnp.bfloat16),) * (1 if whole else 0)
        out_shape += (jax.ShapeDtypeStruct((rows, width // 2), jnp.bfloat16),) * (2 if cut else 0)
        out_shape += (jax.ShapeDtypeStruct((rows, channels), jnp.bfloat16),) * (n_head - 1 if share else 0)
    arrays = [keys, values] + [block[i] for i in range(2) for block in blocks] + [weight, *kept]
    return pl.pallas_call(
        functools.partial(attend_kernel, section, pieces, len(blocks), split, len(kept), n_head if share else 0, cut),
        out_shape=out_shape + (MARK,),
        in_specs=[anywhere] + [vmem] * len(arrays),
        out_specs=(vmem,) * len(out_shape) + (anywhere,),
        scratch_shapes=[pltpu.VMEM((rows, channels), jnp.bfloat16)],
        compiler_params=pltpu.CompilerParams(vmem_limit_bytes=VMEM_LIMIT),
        cost_estimate=pl.CostEstimate(
            flops=2 * rows * channels * (width + 2 * keys.shape[0]),
            bytes_accessed=2 * width * channels,
            transcendentals=rows * keys.shape[0] * channels // HEAD_DIM,
        ),
        name="attend",
    )(mark, *arrays)


def add_kernel(section, n_before, number, mark, *refs):
    @pl.when(lax.axis_index("pipe") == section)
    def _():
        before, terms, out = refs[:n_before], refs[n_before:-2], refs[-2]
        rows = out.shape[0] - sum(block.shape[0] for block in before)
        width = out.shape[1]
        lanes = [slice(0, width) if term.shape[1] == width else slice(number * width, (number + 1) * width) for term in terms]
        total = terms[0][:rows, lanes[0]].astype(jnp.float32)
        for term, columns in zip(terms[1:], lanes[1:]):
            total = total + term[:rows, columns].astype(jnp.float32)
        for block in before:
            out[: block.shape[0], :] = block[...]
        out[out.shape[0] - rows :, :] = total.astype(out.dtype)


def add(section, terms, mark, flops=0, before=(), number=0):
    rows, width = min(term.shape for term in terms)
    rows += sum(block.shape[0] for block in before)
    return pl.pallas_call(
        functools.partial(add_kernel, section, len(before), number),
        out_shape=(jax.ShapeDtypeStruct((rows, width), terms[0].dtype), MARK),
        in_specs=[anywhere] + [vmem] * (len(before) + len(terms)),
        out_specs=(vmem, anywhere),
        compiler_params=pltpu.CompilerParams(vmem_limit_bytes=VMEM_LIMIT),
        cost_estimate=pl.CostEstimate(flops=flops, bytes_accessed=flops // 100, transcendentals=0),
        name="add",
    )(mark, *before, *terms)


def finish_kernel(last, total, second, given, share, *refs):
    shared, out = refs[:-1], refs[-1]
    shape = (out.shape[0], HALF, out.shape[2])
    rows, channels = shared[0].shape
    stage = lax.axis_index("pipe")
    first_half, second_half = (slice(half * HALF, (half + 1) * HALF) for half in range(2))

    @pl.when(stage == last)
    def _():
        out[:, first_half, :] = total[:rows, :].reshape(shape)
        out[:, second_half, :] = total[rows:, :].reshape(shape)

    @pl.when(stage == last - 1)
    def _():
        mine = pl.ds(pl.multiple_of(lax.axis_index("head") * channels, channels), channels)
        value = share[:, mine].astype(jnp.float32)
        for term in shared:
            value = value + term[...].astype(jnp.float32)
        out[:, first_half, :] = value.astype(out.dtype).reshape(shape)
        out[:, second_half, :] = second[rows:, :].reshape(shape)

    @pl.when(stage < last - 1)
    def _():
        out[:, second_half, :] = given[rows:, :].reshape(shape)

        @pl.when(stage % 2 == 0)
        def _():
            out[:, first_half, :] = shared[0][...].reshape(shape)

        @pl.when(stage % 2 == 1)
        def _():
            out[:, first_half, :] = given[:rows, :].reshape(shape)


def finish(last, row_count, total, second, given, share, shared):
    arrays = [total, second, given, share, *shared]
    return pl.pallas_call(
        functools.partial(finish_kernel, last),
        out_shape=jax.ShapeDtypeStruct((row_count, WIN, total.shape[1]), jnp.bfloat16),
        in_specs=[vmem] * len(arrays),
        out_specs=vmem,
        compiler_params=pltpu.CompilerParams(vmem_limit_bytes=VMEM_LIMIT),
        name="finish",
    )(*arrays)


def new_mark():
    return pl.pallas_call(
        lambda ref: None,
        out_shape=MARK,
        out_specs=anywhere,
        compiler_params=pltpu.CompilerParams(vmem_limit_bytes=1024 * 1024),
        name="new_mark",
    )()


def after(arrays, *marks, flops=0):
    shapes = tuple(jax.ShapeDtypeStruct(array.shape, array.dtype) for array in arrays)
    return pl.pallas_call(
        lambda *refs: None,
        out_shape=shapes,
        in_specs=[anywhere] * (len(arrays) + len(marks)),
        out_specs=(anywhere,) * len(arrays),
        input_output_aliases={place: place for place in range(len(arrays))},
        compiler_params=pltpu.CompilerParams(vmem_limit_bytes=1024 * 1024),
        cost_estimate=pl.CostEstimate(flops=flops, bytes_accessed=flops // 100, transcendentals=0),
        name="after",
    )(*arrays, *marks)


def per_device(stream, score_scale, value_weight, out_weight):
    row_count, col_count, width = stream.shape
    assert col_count == WIN, "one window"
    sections, n_win, n_head = (lax.axis_size(axis) for axis in AXES)
    assert sections % 2 == 0, "section pairs"
    value_cols, out_rows = value_weight[0], out_weight[0]
    places = [(win, group) for win in range(n_win) for group in range(n_head)]

    def send(value, start, stop, over=0, turn=0):
        return send_all(value, [(start, stop, over, turn)])

    def send_all(value, hops):
        at = lambda pipe, win, group: (pipe * n_win + win % n_win) * n_head + group % n_head
        pairs = [
            (at(start, win, group), at(stop, win + over, group + turn))
            for start, stop, over, turn in hops
            for win, group in places
        ]
        return lax.ppermute(value, AXES, pairs)

    piece = row_count * HALF
    natural = tuple(
        (chunk % 2) * row_count + chunk // 2 for chunk in range(row_count * col_count // HALF)
    )
    own = stream.reshape(row_count * col_count, width)
    arrived = [own] + [send(own, 0, 0, 0, turn) for turn in range(1, n_head)]
    mark = new_mark()
    blocks, filled = [], ()
    for turn, cells in enumerate(arrived):
        *block, mark = project(
            0, natural, [[cells]], mark, score_scale, value_cols, turn * own.shape[0], n_head * own.shape[0], filled
        )
        blocks.append(block)
        filled = block[2:]
    halves = [[(block, half * piece, piece) for block in range(n_head)] for half in range(2)]
    straight = tuple(range(row_count * n_head))
    kept = None

    for section in range(sections):
        shift = section % 2
        last = section + 1 == sections
        idle = (section + 2) % sections
        moved = []
        for half in range(2):
            share = section + 2 == sections and not half
            carried = [kept] if share or last and half else []
            if last and half:
                (mark,) = after([mark], given, *early)
            cut = shift == 1 and half == 1 and not last
            whole = not cut
            *part, mark = attend(
                section, halves[half], blocks, filled, mark, out_rows, last, carried, share, cut, whole
            )
            if share:
                own_share, *shared = part
            cross = 0 if half else shift if last else 1 if shift else -1
            if last and half:
                terms = [send(part[turn], section, section - 1, 0, turn) for turn in range(1, n_head)]
                terms += [send(part[0], section, section - 1)]
            elif last:
                terms = [send(part[turn], section, section - 1, cross, turn) for turn in range(n_head)]
            elif shift and not half:
                terms = [send(block, section, idle, cross) for block in part]
            elif shift:
                terms = [[send(block, section, section - 1, 0, turn) for turn in range(n_head)] for block in part]
            else:
                terms = [[send(part[0], section, section + 1, cross, turn)] for turn in range(n_head)]
            moved.append(terms)
        if shift and not last:
            arrived = [after([block], mark, flops=0)[0] for block in moved[0]]
            moved[0] = [
                [send(block, idle, section + 1, 0, turn) for block in arrived] for turn in range(n_head)
            ]
            sums = []
            for number, terms in enumerate(moved[1]):
                total, mark = add(section - 1, terms, mark, 4 * 10**9 if number else 0)
                sums.append(send(total, section - 1, section + 1))
            moved[1] = [sums]
        if section + 2 == sections:
            straight_back = [(source, source - 1, 0, 0) for source in range(1, section + 1)]
            across = [(source, source - 1, 1, 0) for source in range(1, section, 2)]
            *shared, early_kept = after([*shared, kept], mark)
            early = [
                send_all(block, ([] if turn else across) + [(section, section, 0, turn + 1)])
                for turn, block in enumerate(shared)
            ]
            given = send_all(early_kept, straight_back)
            kept = None
        if not last:
            blocks, filled, rows = [None, None], (), piece * n_head
            for half in (1, 0) if shift else (0, 1):
                keep_rows = 2 * rows if section + 2 < sections else half * rows
                *block, mark = project(
                    section + 1,
                    straight,
                    moved[half],
                    mark,
                    score_scale,
                    value_cols,
                    half * rows,
                    2 * rows,
                    filled,
                    kept,
                    keep_rows,
                )
                if keep_rows:
                    *block, kept = block
                blocks[half] = block
                filled = block[2:]
            halves = [[(0, 0, piece * n_head)], [(1, 0, piece * n_head)]]
    *across, mark = after([*moved[0][1:], mark])
    first, mark = add(sections - 2, [moved[0][0], *across], mark, 4 * 10**9)
    second, mark = add(sections - 2, moved[1][:-1], mark, 4 * 10**9)
    total, mark = add(sections - 2, [second, moved[1][-1]], mark, 0, (first,))
    total = send(total, sections - 2, sections - 1)
    return finish(sections - 1, row_count * n_head, total, moved[1][-1], given, own_share, early)[None]


def solution(mesh):
    placed = (
        P("head", "win", None),
        P("pipe", None),
        P("pipe", None, "head"),
        P("pipe", "head", None),
    )
    return jax.shard_map(
        per_device,
        mesh=mesh,
        in_specs=placed,
        out_specs=P("pipe", None, "win", "head"),
        check_vma=False,
    )
```

```python
import functools
import math

import jax
import jax.numpy as jnp
from jax import lax
from jax.experimental import pallas as pl
from jax.experimental.pallas import tpu as pltpu
from jax.sharding import PartitionSpec as P

HEAD_DIM = 128
WIN = 32
HALF = WIN // 2
EPSILON = 1e-06
AXES = ("pipe", "win", "head")
VMEM_LIMIT = 14 * 1024 * 1024

vmem = pl.BlockSpec(memory_space=pltpu.VMEM)
anywhere = pl.BlockSpec(memory_space=pl.ANY)
MARK = jax.ShapeDtypeStruct((8, 128), jnp.float32)


def project_kernel(section, chunk_order, counts, n_filled, first_row, keep_row, mark, *refs):
    parts = []
    for count in counts:
        parts.append(refs[:count])
        refs = refs[count:]
    scale, weight = refs[:2]
    x_ref, q_ref, k_ref, v_ref, *kept, _ = refs[2 + n_filled :]
    channels = q_ref.shape[1]
    rows_here = len(chunk_order) * HALF

    @pl.when(lax.axis_index("pipe") == section)
    def _():
        mine = pl.ds(pl.multiple_of(lax.axis_index("head") * channels, channels), channels)
        inverse = [None] * len(chunk_order)
        for source, target in enumerate(chunk_order):
            rows = pl.ds(source * HALF, HALF)
            put = pl.ds(target * HALF, HALF)
            total = None
            for part in parts:
                term = join([columns[rows, :].astype(jnp.float32) for columns in part], 1)
                total = term if total is None else total + term
            x = total.astype(x_ref.dtype)
            x_ref[put, :] = x
            wide = x.astype(jnp.float32)
            mean_square = jnp.mean(wide * wide, axis=1, keepdims=True)
            inverse[target] = lax.rsqrt(mean_square + EPSILON)
        inverse = jnp.concatenate(inverse, axis=0)
        here = slice(first_row, first_row + rows_here)
        values = jnp.dot(x_ref[...], weight[...], preferred_element_type=jnp.float32)
        v_ref[here, :] = (values * inverse).astype(v_ref.dtype)
        key = (x_ref[:, mine].astype(jnp.float32) * inverse).astype(k_ref.dtype)
        k_ref[here, :] = key
        q_ref[...] = (key.astype(jnp.float32) * scale[:, mine]).astype(q_ref.dtype)
        for target in kept:
            target[keep_row : keep_row + rows_here, :] = x_ref[:, mine]


def project(section, chunk_order, parts, mark, scale, weight, first_row, total_rows, filled, kept=None, keep_rows=0):
    rows, (width, channels) = parts[0][0].shape[0], weight.shape
    shapes = [(rows, width), (rows, channels)] + [(total_rows, channels)] * 2
    shapes += [(keep_rows, channels)] if keep_rows else []
    counts = [len(part) for part in parts]
    arrays = [block for part in parts for block in part] + [scale, weight, *filled] + ([] if kept is None else [kept])
    at = 1 + sum(counts) + 2
    aliases = {at: 2, at + 1: 3} if filled else {}
    if kept is not None:
        aliases[len(arrays)] = 4
    keep_row = first_row if keep_rows > rows else 0
    return pl.pallas_call(
        functools.partial(
            project_kernel, section, chunk_order, counts, len(arrays) - at + 1, first_row, keep_row
        ),
        out_shape=tuple(jax.ShapeDtypeStruct(shape, jnp.bfloat16) for shape in shapes) + (MARK,),
        in_specs=[anywhere] + [vmem] * len(arrays),
        out_specs=(vmem,) * len(shapes) + (anywhere,),
        input_output_aliases=aliases,
        compiler_params=pltpu.CompilerParams(vmem_limit_bytes=VMEM_LIMIT),
        cost_estimate=pl.CostEstimate(
            flops=2 * rows * width * channels, bytes_accessed=2 * width * channels, transcendentals=0
        ),
        name="project",
    )(mark, *arrays)


def join(values, axis):
    return jnp.concatenate(values, axis=axis) if len(values) > 1 else values[0]


def attend_kernel(section, pieces, n_blocks, split, carry, copies, cut, mark, k, v, *refs):
    xs, qs, refs = refs[:n_blocks], refs[n_blocks : 2 * n_blocks], refs[2 * n_blocks :]
    weight, refs = refs[0], refs[1:]
    kept, refs = refs[:carry], refs[carry:]
    outs, o_ref = refs[:-2], refs[-1]
    channels = qs[0].shape[1]
    width = xs[0].shape[1]
    inv_root = 1.0 / math.sqrt(HEAD_DIM)
    n_head = width // channels

    @pl.when(lax.axis_index("pipe") == section)
    def _():
        heads = [slice(at, at + HEAD_DIM) for at in range(0, channels, HEAD_DIM)]
        ones = jnp.ones((v.shape[0], HEAD_DIM), jnp.bfloat16)
        weights = []
        for lanes in heads:
            q = join([qs[block][start : start + size, lanes] for block, start, size in pieces], 0)
            scores = lax.dot_general(
                q, k[:, lanes], (((1,), (1,)), ((), ())), preferred_element_type=jnp.float32
            )
            highest = jnp.max(scores, axis=1, keepdims=True)
            weights.append(jnp.exp2((scores - highest) * (inv_root * math.log2(math.e))).astype(jnp.bfloat16))
        for lanes, weight_of_head in zip(heads, weights):
            values = jnp.concatenate([v[:, lanes], ones], axis=1)
            attended = jnp.dot(weight_of_head, values, preferred_element_type=jnp.float32)
            o_ref[:, lanes] = (attended[:, :HEAD_DIM] / attended[:, HEAD_DIM:]).astype(o_ref.dtype)
        mine = jnp.where(lax.axis_index("head") == 0, 1.0, 0.0)
        attended = o_ref[...]
        step = channels if split else min(512, width)
        for column in range(0, width, step):
            if split:
                out = outs[column // step]
                block = lax.rem(lax.axis_index("head") + column // step, n_head)
                lanes = pl.ds(pl.multiple_of(block * step, step), step)
                put_lanes = slice(0, step)
            else:
                out = outs[0]
                lanes = put_lanes = slice(column, column + step)
                if cut:
                    part = column * 2 // width
                    cut_out, cut_lanes = outs[len(outs) - 2 + part], slice(column - part * width // 2, column - part * width // 2 + step)
            g = jnp.dot(attended, weight[:, lanes], preferred_element_type=jnp.float32)
            at = 0
            for turn, (block, start, size) in enumerate(pieces):
                residual = xs[block][start : start + size, lanes].astype(jnp.float32) * mine
                value = residual + g[at : at + size]
                if len(pieces) > 1:
                    place = lax.rem(lax.axis_index("head") + len(pieces) - turn, len(pieces)) * size
                    rows = pl.ds(pl.multiple_of(place, size), size)
                else:
                    rows = slice(0, size)
                value = value.astype(out.dtype)
                if len(outs) != 2 or not cut:
                    out[rows, put_lanes] = value
                if cut:
                    cut_out[rows, cut_lanes] = value
                at += size
        for turn in range(1, copies):
            block = lax.rem(lax.axis_index("head") + turn, n_head)
            lanes = pl.ds(pl.multiple_of(block * channels, channels), channels)
            outs[turn][...] = outs[0][:, lanes]

    if copies:

        @pl.when(lax.axis_index("pipe") != section)
        def _():
            outs[1][...] = kept[0][: o_ref.shape[0], :]

    elif carry:
        outs[0][o_ref.shape[0] :, :] = kept[0][...]


def attend(section, pieces, blocks, filled, mark, weight, split, kept=(), share=False, cut=False, whole=True):
    rows = sum(size for _, _, size in pieces)
    channels, width = weight.shape
    keys, values = filled
    n_head = width // channels
    if split:
        out_shape = tuple(
            jax.ShapeDtypeStruct((rows * (2 if kept and turn == 0 else 1), channels), jnp.bfloat16)
            for turn in range(n_head)
        )
    else:
        out_shape = (jax.ShapeDtypeStruct((rows, width), jnp.bfloat16),) * (1 if whole else 0)
        out_shape += (jax.ShapeDtypeStruct((rows, width // 2), jnp.bfloat16),) * (2 if cut else 0)
        out_shape += (jax.ShapeDtypeStruct((rows, channels), jnp.bfloat16),) * (n_head - 1 if share else 0)
    arrays = [keys, values] + [block[i] for i in range(2) for block in blocks] + [weight, *kept]
    return pl.pallas_call(
        functools.partial(attend_kernel, section, pieces, len(blocks), split, len(kept), n_head if share else 0, cut),
        out_shape=out_shape + (MARK,),
        in_specs=[anywhere] + [vmem] * len(arrays),
        out_specs=(vmem,) * len(out_shape) + (anywhere,),
        scratch_shapes=[pltpu.VMEM((rows, channels), jnp.bfloat16)],
        compiler_params=pltpu.CompilerParams(vmem_limit_bytes=VMEM_LIMIT),
        cost_estimate=pl.CostEstimate(
            flops=2 * rows * channels * (width + 2 * keys.shape[0]),
            bytes_accessed=2 * width * channels,
            transcendentals=rows * keys.shape[0] * channels // HEAD_DIM,
        ),
        name="attend",
    )(mark, *arrays)


def add_kernel(section, n_before, number, mark, *refs):
    @pl.when(lax.axis_index("pipe") == section)
    def _():
        before, terms, out = refs[:n_before], refs[n_before:-2], refs[-2]
        rows = out.shape[0] - sum(block.shape[0] for block in before)
        width = out.shape[1]
        lanes = [slice(0, width) if term.shape[1] == width else slice(number * width, (number + 1) * width) for term in terms]
        total = terms[0][:rows, lanes[0]].astype(jnp.float32)
        for term, columns in zip(terms[1:], lanes[1:]):
            total = total + term[:rows, columns].astype(jnp.float32)
        for block in before:
            out[: block.shape[0], :] = block[...]
        out[out.shape[0] - rows :, :] = total.astype(out.dtype)


def add(section, terms, mark, flops=0, before=(), number=0):
    rows, width = min(term.shape for term in terms)
    rows += sum(block.shape[0] for block in before)
    return pl.pallas_call(
        functools.partial(add_kernel, section, len(before), number),
        out_shape=(jax.ShapeDtypeStruct((rows, width), terms[0].dtype), MARK),
        in_specs=[anywhere] + [vmem] * (len(before) + len(terms)),
        out_specs=(vmem, anywhere),
        compiler_params=pltpu.CompilerParams(vmem_limit_bytes=VMEM_LIMIT),
        cost_estimate=pl.CostEstimate(flops=flops, bytes_accessed=flops // 100, transcendentals=0),
        name="add",
    )(mark, *before, *terms)


def finish_kernel(last, total, second, given, share, *refs):
    shared, out = refs[:-1], refs[-1]
    shape = (out.shape[0], HALF, out.shape[2])
    rows, channels = shared[0].shape
    stage = lax.axis_index("pipe")
    first_half, second_half = (slice(half * HALF, (half + 1) * HALF) for half in range(2))

    @pl.when(stage == last)
    def _():
        out[:, first_half, :] = total[:rows, :].reshape(shape)
        out[:, second_half, :] = total[rows:, :].reshape(shape)

    @pl.when(stage == last - 1)
    def _():
        mine = pl.ds(pl.multiple_of(lax.axis_index("head") * channels, channels), channels)
        value = share[:, mine].astype(jnp.float32)
        for term in shared:
            value = value + term[...].astype(jnp.float32)
        out[:, first_half, :] = value.astype(out.dtype).reshape(shape)
        out[:, second_half, :] = second[rows:, :].reshape(shape)

    @pl.when(stage < last - 1)
    def _():
        out[:, second_half, :] = given[rows:, :].reshape(shape)

        @pl.when(stage % 2 == 0)
        def _():
            out[:, first_half, :] = shared[0][...].reshape(shape)

        @pl.when(stage % 2 == 1)
        def _():
            out[:, first_half, :] = given[:rows, :].reshape(shape)


def finish(last, row_count, total, second, given, share, shared):
    arrays = [total, second, given, share, *shared]
    return pl.pallas_call(
        functools.partial(finish_kernel, last),
        out_shape=jax.ShapeDtypeStruct((row_count, WIN, total.shape[1]), jnp.bfloat16),
        in_specs=[vmem] * len(arrays),
        out_specs=vmem,
        compiler_params=pltpu.CompilerParams(vmem_limit_bytes=VMEM_LIMIT),
        name="finish",
    )(*arrays)


def new_mark():
    return pl.pallas_call(
        lambda ref: None,
        out_shape=MARK,
        out_specs=anywhere,
        compiler_params=pltpu.CompilerParams(vmem_limit_bytes=1024 * 1024),
        name="new_mark",
    )()


def after(arrays, *marks, flops=0):
    shapes = tuple(jax.ShapeDtypeStruct(array.shape, array.dtype) for array in arrays)
    return pl.pallas_call(
        lambda *refs: None,
        out_shape=shapes,
        in_specs=[anywhere] * (len(arrays) + len(marks)),
        out_specs=(anywhere,) * len(arrays),
        input_output_aliases={place: place for place in range(len(arrays))},
        compiler_params=pltpu.CompilerParams(vmem_limit_bytes=1024 * 1024),
        cost_estimate=pl.CostEstimate(flops=flops, bytes_accessed=flops // 100, transcendentals=0),
        name="after",
    )(*arrays, *marks)


def per_device(stream, score_scale, value_weight, out_weight):
    row_count, col_count, width = stream.shape
    assert col_count == WIN, "one window"
    sections, n_win, n_head = (lax.axis_size(axis) for axis in AXES)
    assert sections % 2 == 0, "section pairs"
    value_cols, out_rows = value_weight[0], out_weight[0]
    places = [(win, group) for win in range(n_win) for group in range(n_head)]

    def send(value, start, stop, over=0, turn=0):
        return send_all(value, [(start, stop, over, turn)])

    def send_all(value, hops):
        at = lambda pipe, win, group: (pipe * n_win + win % n_win) * n_head + group % n_head
        pairs = [
            (at(start, win, group), at(stop, win + over, group + turn))
            for start, stop, over, turn in hops
            for win, group in places
        ]
        return lax.ppermute(value, AXES, pairs)

    piece = row_count * HALF
    natural = tuple(
        (chunk % 2) * row_count + chunk // 2 for chunk in range(row_count * col_count // HALF)
    )
    own = stream.reshape(row_count * col_count, width)
    arrived = [own] + [send(own, 0, 0, 0, turn) for turn in range(1, n_head)]
    mark = new_mark()
    blocks, filled = [], ()
    for turn, cells in enumerate(arrived):
        *block, mark = project(
            0, natural, [[cells]], mark, score_scale, value_cols, turn * own.shape[0], n_head * own.shape[0], filled
        )
        blocks.append(block)
        filled = block[2:]
    halves = [[(block, half * piece, piece) for block in range(n_head)] for half in range(2)]
    straight = tuple(range(row_count * n_head))
    kept = None

    for section in range(sections):
        shift = section % 2
        last = section + 1 == sections
        idle = (section + 2) % sections
        moved = []
        for half in range(2):
            share = section + 2 == sections and not half
            carried = [kept] if share or last and half else []
            if last and half:
                (mark,) = after([mark], given, *early)
            cut = shift == 1 and half == 1 and not last
            whole = not cut
            *part, mark = attend(
                section, halves[half], blocks, filled, mark, out_rows, last, carried, share, cut, whole
            )
            if share:
                own_share, *shared = part
            cross = 0 if half else shift if last else 1 if shift else -1
            if last and half:
                terms = [send(part[turn], section, section - 1, 0, turn) for turn in range(1, n_head)]
                terms += [send(part[0], section, section - 1)]
            elif last:
                terms = [send(part[turn], section, section - 1, cross, turn) for turn in range(n_head)]
            elif shift and not half:
                terms = [send(block, section, idle, cross) for block in part]
            elif shift:
                terms = [[send(block, section, section - 1, 0, turn) for turn in range(n_head)] for block in part]
            else:
                terms = [[send(part[0], section, section + 1, cross, turn)] for turn in range(n_head)]
            moved.append(terms)
        if shift and not last:
            arrived = [after([block], mark, flops=0)[0] for block in moved[0]]
            moved[0] = [
                [send(block, idle, section + 1, 0, turn) for block in arrived] for turn in range(n_head)
            ]
            sums = []
            for number, terms in enumerate(moved[1]):
                total, mark = add(section - 1, terms, mark, 4 * 10**9 if number else 0)
                sums.append(send(total, section - 1, section + 1))
            moved[1] = [sums]
        if section + 2 == sections:
            straight_back = [(source, source - 1, 0, 0) for source in range(1, section + 1)]
            across = [(source, source - 1, 1, 0) for source in range(1, section, 2)]
            *shared, early_kept = after([*shared, kept], mark)
            early = [
                send_all(block, ([] if turn else across) + [(section, section, 0, turn + 1)])
                for turn, block in enumerate(shared)
            ]
            given = send_all(early_kept, straight_back)
            kept = None
        if not last:
            blocks, filled, rows = [None, None], (), piece * n_head
            for half in (1, 0) if shift else (0, 1):
                keep_rows = 2 * rows if section + 2 < sections else half * rows
                *block, mark = project(
                    section + 1,
                    straight,
                    moved[half],
                    mark,
                    score_scale,
                    value_cols,
                    half * rows,
                    2 * rows,
                    filled,
                    kept,
                    keep_rows,
                )
                if keep_rows:
                    *block, kept = block
                blocks[half] = block
                filled = block[2:]
            halves = [[(0, 0, piece * n_head)], [(1, 0, piece * n_head)]]
    *across, mark = after([*moved[0][1:], mark])
    first, mark = add(sections - 2, [moved[0][0], *across], mark, 4 * 10**9)
    second, mark = add(sections - 2, moved[1][:-1], mark, 4 * 10**9)
    total, mark = add(sections - 2, [second, moved[1][-1]], mark, 0, (first,))
    total = send(total, sections - 2, sections - 1)
    return finish(sections - 1, row_count * n_head, total, moved[1][-1], given, own_share, early)[None]


def solution(mesh):
    placed = (
        P("head", "win", None),
        P("pipe", None),
        P("pipe", None, "head"),
        P("pipe", "head", None),
    )
    return jax.shard_map(
        per_device,
        mesh=mesh,
        in_specs=placed,
        out_specs=P("pipe", None, "win", "head"),
        check_vma=False,
    )
```
